256 devices in a mesh: region: 32 (over x, y, core), local: 8 (over z).
Axes of the slice: x: 4, y: 4, z: 8, core: 2. Of those that a mesh axis runs over, the one named last changes fastest.
Arguments:
- tokens: bfloat16 [4096, 7168], P('region', 'local'), may hold values from -44 to 44
- norm_gain: float32 [7168], P('local'), may hold values from 0.1 to 1.9
- w_gate: bfloat16 [32, 7168, 2048], P('region', None, 'local'), may hold values from -0.0625 to 0.0625
- w_up: bfloat16 [32, 7168, 2048], P('region', None, 'local'), may hold values from -0.0625 to 0.0625
- w_down: bfloat16 [32, 2048, 7168], P('region', 'local'), may hold values from -0.125 to 0.125
- regions: int32 [4096, 2], P('region'), may hold values from 0 to 31, all different within a row; in each aligned block of 128 rows (0 to 127, 128 to 255, ...) at most 10 rows name the same one
- combine: float32 [4096, 2], P('region'), may hold values from 0.1 to 1
- grad_out: bfloat16 [4096, 7168], P('region', 'local'), may hold values from -3 to 3
Outputs:
- moe_out: bfloat16 [4096, 7168], P('region', 'local')
- grad_tokens: bfloat16 [4096, 7168], P('region', 'local')
- grad_combine: float32 [4096, 2], P('region')
The draws below stay inside these ranges and needn't reach their ends.
Inputs may be any that keep to these rules, and one draw needn't show every extreme that they name: `regions`: each row names 2 different experts; among the rows of one device (aligned blocks of 128 rows) no expert is named by more than 10 rows, a bound that some block reaches.
All inputs are finite; a program needn't handle non-finite values.
Results may differ from the reference program's by a relative error of at most 0.02.
Values may be sent and summed in bfloat16 or wider, within the bound.
No kernel may reach another device: no remote copies, remote signals or barrier semaphores. Data moves between devices by JAX's collectives and lax.ppermute only.
A program may use at most 128 MiB of HBM per device.

```python
import math
import jax
import jax.numpy as jnp
import numpy as np
from jax import lax

D = 7168
HID = 2048
TOP = 2
T_DEV = 128
TOKENS = 4096
EXPERTS = 32
CAP = 10
N_REGION = 32


def draw_tokens(key, part):
    key_base, key_cols, key_rows = jax.random.split(key, 3)
    position = jnp.arange(D, dtype=jnp.float32) / D
    roughness = jnp.exp(jax.random.uniform(key_cols, (D,), jnp.float32, -0.7, 0.7))
    column_scale = 0.6 * jnp.power(3.0, position) * roughness
    row_scale = jnp.exp(jax.random.uniform(key_rows, (TOKENS, 1), jnp.float32, math.log(0.3), math.log(3.0)))
    base = jnp.clip(jax.random.normal(key_base, (TOKENS, D), jnp.float32), -4.0, 4.0)
    return (base * column_scale * row_scale).astype(jnp.bfloat16)


def block_levels(rng, extent, shards, least, largest):
    gain, own = 1.0, jax.random.fold_in(rng, 6)
    for axis_at, blocks in shards:
        heights = jnp.exp(jax.random.uniform(jax.random.fold_in(own, axis_at), (blocks,), jnp.float32, least / len(shards), largest / len(shards)))
        gain = gain * jnp.repeat(heights, extent[axis_at] // blocks).reshape([-1 if axis == axis_at else 1 for axis in range(len(extent))])
    return gain


def shared_out(rng, own, number, rows, count, top, reach, lean):
    order = jax.random.permutation(rng, count)
    heavy_load, common = load_shares(count, rows * top, reach, lean, True), load_shares(count, rows * top, reach, lean, False)
    places = jnp.arange(count)

    def named(lengths, offset_by):
        used = int((lengths > 0).sum())
        fixed = max(1, used // 4)
        moved = fixed + (places - fixed + offset_by * (used - fixed)) % max(1, count - fixed)
        return jnp.zeros((count,), jnp.int32).at[order[jnp.where(places < fixed, places, moved)]].set(jnp.asarray(lengths, jnp.int32))

    lengths = jnp.where(number % 4 == 0, named(heavy_load, number // 4), named(common, number - number // 4 - 1))
    mixed = jax.random.permutation(jax.random.fold_in(own, 3), count)
    source_of, sink = mixed[0:count // 2 * 2:2], mixed[1:count // 2 * 2:2]
    margin = jnp.minimum(lengths[source_of] - 1, reach - lengths[sink]) // 2
    margin = jnp.where((source_of == order[0]) | (sink == order[0]) | (lengths[sink] == 0), 0, jnp.maximum(margin, 0))
    moved = jax.random.randint(jax.random.fold_in(own, 4), (count // 2,), 0, 1 << 20) % (margin + 1)
    lengths = lengths.at[source_of].add(-moved).at[sink].add(moved)
    members = jnp.searchsorted(jnp.cumsum(lengths), jnp.arange(rows * top), side="right").astype(jnp.int32)
    grid = members.reshape(top, rows).T
    grid = grid[jax.random.permutation(jax.random.fold_in(own, 1), rows)]
    offset_by = jax.random.randint(jax.random.fold_in(own, 2), (rows, 1), 0, top)
    return jnp.take_along_axis(grid, (jnp.arange(top)[None, :] + offset_by) % top, axis=1)


def load_shares(count, total, reach, slope, full):
    portions = [(1 << 20) // math.isqrt(standing ** slope) + 1 for standing in range(1, count + 1)]
    largest = reach if full else min(reach, max(-(-total // count), total * portions[0] // sum(portions)))
    least = 1 if total - largest >= count - 1 else 0
    counts, rest = [largest] + [least] * (count - 1), total - largest - least * (count - 1)
    while rest > 0:
        movable = [i for i in range(1, count) if counts[i] < largest] or [i for i in range(1, count) if counts[i] < reach]
        whole, budget = sum([portions[i] for i in movable]), rest
        for i in movable:
            extra = min(reach - counts[i], max(1, budget * portions[i] // whole), rest)
            counts[i] = counts[i] + extra
            rest = rest - extra
    return np.array(counts)


def bell_draw(stream_key, dims, width, limit, cuts=(), kind=jnp.bfloat16):
    array = jax.random.normal(stream_key, dims, jnp.float32) * width
    if len(cuts) > 0:
        array = block_levels(stream_key, dims, cuts, -0.22, 0.18) * array
    return jnp.clip(array, min=-limit, max=limit).astype(kind)


def setup_inputs(seed: int = 0) -> dict:
    streams_of = jax.random.split(jax.random.key(seed), 9)
    tokens = draw_tokens(jax.random.fold_in(streams_of[8], 71), 0)
    norm_gain = jnp.clip(1.0 + 0.18 * jax.random.normal(streams_of[1], (D,), jnp.float32), 0.1, 1.9)
    w_gate = bell_draw(streams_of[2], (EXPERTS, D, HID), D ** -0.5, 0.0625, ((0, 32), (2, 8)))
    w_up = bell_draw(streams_of[3], (EXPERTS, D, HID), D ** -0.5, 0.0625, ((0, 32), (2, 8)))
    w_down = bell_draw(streams_of[4], (EXPERTS, HID, D), HID ** -0.5, 0.125, ((0, 32), (1, 8)))
    regions_keys = jax.random.split(jax.random.fold_in(streams_of[5], 1), TOKENS // T_DEV)
    regions_turns = jax.random.permutation(jax.random.fold_in(streams_of[5], 3), TOKENS // T_DEV)
    regions = jax.vmap(lambda own, number: shared_out(jax.random.fold_in(streams_of[5], 2), own, number, T_DEV, N_REGION, TOP, CAP, 2))(regions_keys, regions_turns).reshape((TOKENS, TOP))
    combine = jnp.clip(jnp.exp(math.log(1.0) - 2.3025851 * jax.random.uniform(streams_of[6], (TOKENS, TOP), jnp.float32) ** block_levels(streams_of[6], (TOKENS, TOP), ((0, 32),), -0.2, 0.2)), 0.1, 1.0)
    grad_out = bell_draw(streams_of[7], (TOKENS, D), 0.5, 3.0, ((0, 32), (1, 8)))
    return dict(tokens=tokens, norm_gain=norm_gain, w_gate=w_gate, w_up=w_up, w_down=w_down, regions=regions, combine=combine, grad_out=grad_out)


def reference(tokens, norm_gain, w_gate, w_up, w_down, regions, combine, grad_out):
    inputs_f32 = tokens.astype(jnp.float32)
    sum_squares = lax.optimization_barrier(jnp.sum(inputs_f32 * inputs_f32, axis=1, keepdims=True))
    inv_rms = lax.rsqrt(sum_squares / D + 1e-06)
    gain_f32 = norm_gain.astype(jnp.float32)
    normed = (inputs_f32 * inv_rms * gain_f32).astype(jnp.bfloat16)
    flat_routes = regions.reshape(-1)
    flat_weights = combine.reshape(-1)
    most_rows = N_REGION * CAP

    def one_expert(expert, carry):
        out_total, grad_total, comb_total = carry
        chosen = flat_routes == expert
        index = jnp.nonzero(chosen, size=most_rows, fill_value=0)[0].astype(jnp.int32)
        live = (jnp.arange(most_rows) < jnp.sum(chosen.astype(jnp.int32))).astype(jnp.float32)
        owner = index // TOP
        rows_in = normed[owner]
        rows_grad = grad_out[owner]
        gate_w = w_gate[expert]
        up_w = w_up[expert]
        down_w = w_down[expert]
        gate_pre = jnp.dot(rows_in, gate_w, preferred_element_type=jnp.float32)
        up_pre = jnp.dot(rows_in, up_w, preferred_element_type=jnp.float32)
        sig_gate = jax.nn.sigmoid(gate_pre)
        act_gate = gate_pre * sig_gate
        hidden = (act_gate * up_pre).astype(jnp.bfloat16)
        expert_out = jnp.dot(hidden, down_w, preferred_element_type=jnp.float32)
        grad_hidden = jnp.dot(rows_grad, down_w.T, preferred_element_type=jnp.float32)
        grad_gate = (grad_hidden * up_pre * sig_gate * (1.0 + gate_pre * (1.0 - sig_gate))).astype(jnp.bfloat16)
        grad_up = (grad_hidden * act_gate).astype(jnp.bfloat16)
        branch_grad = jnp.dot(grad_gate, gate_w.T, preferred_element_type=jnp.float32) + jnp.dot(grad_up, up_w.T, preferred_element_type=jnp.float32)
        weight_live = flat_weights[index] * live
        out_total = out_total.at[owner].add(weight_live[:, None] * expert_out)
        grad_total = grad_total.at[owner].add(weight_live[:, None] * branch_grad)
        comb_piece = lax.optimization_barrier(jnp.sum(rows_grad.astype(jnp.float32) * expert_out, axis=1)) * live
        comb_total = comb_total.at[index].add(comb_piece)
        return (out_total, grad_total, comb_total)
    start = (jnp.zeros((TOKENS, D), jnp.float32), jnp.zeros((TOKENS, D), jnp.float32), jnp.zeros((TOKENS * TOP,), jnp.float32))
    out_total, grad_total, comb_total = lax.fori_loop(0, N_REGION, one_expert, start)
    moe_out = out_total.astype(jnp.bfloat16)
    scaled = gain_f32 * grad_total
    inner = lax.optimization_barrier(jnp.sum(inputs_f32 * scaled, axis=1, keepdims=True))
    grad_tokens = (inv_rms * scaled - inputs_f32 * inv_rms * inv_rms * inv_rms * inner / D).astype(jnp.bfloat16)
    grad_combine = comb_total.reshape(TOKENS, TOP)
    return (moe_out, grad_tokens, grad_combine)
```

```python
import functools

import jax
import jax.numpy as jnp
from jax import lax
from jax.experimental import pallas as pl
from jax.experimental.pallas import tpu as pltpu
from jax.sharding import PartitionSpec as P

BF = jnp.bfloat16
F32 = jnp.float32
NT = (((1,), (1,)), ((), ()))
TN = (((0,), (0,)), ((), ()))
VMEM_LIMIT = 48 * 1024 * 1024


def fold_lanes(width):
    return 128 * -(-width // 256)


def packed_lanes(width):
    return 2 * width + fold_lanes(width)


def dot(a, b, dims=(((1,), (0,)), ((), ())), precision=None):
    return lax.dot_general(a, b, dims, precision=precision, preferred_element_type=F32)


def params(**kw):
    return pltpu.CompilerParams(vmem_limit_bytes=VMEM_LIMIT, **kw)


def fold_matrix(regions):
    rows = 8 * regions
    i = lax.broadcasted_iota(jnp.int32, (rows, rows), 0)
    j = lax.broadcasted_iota(jnp.int32, (rows, rows), 1)
    return (j == 4 * (i % (2 * regions)) + i // (2 * regions)).astype(BF)


def encode(main, rest, fold):
    width = main.shape[1] // 2
    lanes = fold_lanes(width)
    pad = 2 * lanes - width
    parts = []
    for side in range(2):
        parts.append(rest[:, side * width : side * width + lanes])
        tail = rest[:, side * width + lanes : (side + 1) * width]
        if pad:
            tail = jnp.concatenate([tail, jnp.zeros((rest.shape[0], pad), rest.dtype)], axis=1)
        parts.append(tail)
    stacked = jnp.concatenate(parts, axis=0)
    return jnp.concatenate([main, dot(fold, stacked, TN).astype(BF)], axis=1)


def decode(block, width, fold):
    lanes = fold_lanes(width)
    rows = block.shape[0]
    rest = dot(fold, block[:, 2 * width :]).astype(BF)
    few = rows // 4
    sides = []
    for side in range(2):
        head = rest[(2 * side) * few : (2 * side + 1) * few]
        tail = rest[(2 * side + 1) * few : (2 * side + 2) * few, : width - lanes]
        low = jnp.concatenate([head, tail], axis=1)
        sides.append(jnp.concatenate([block[:, side * width : (side + 1) * width], low], axis=0))
    return sides


def slot_ids(regions, tokens):
    s = lax.broadcasted_iota(jnp.int32, (10 * regions, tokens), 0)
    late = s - 8 * regions
    expert = jnp.where(late < 0, s // 8, late // 2)
    slot = jnp.where(late < 0, s % 8, 8 + late % 2)
    return expert, slot


def ranks(named):
    count = named.shape[1]
    before = lax.broadcasted_iota(jnp.int32, (count, count), 0)
    after = lax.broadcasted_iota(jnp.int32, (count, count), 1)
    return dot(named.astype(F32).astype(BF), (before < after).astype(F32).astype(BF))


def placed(routes, regions):
    expert, slot = slot_ids(regions, routes.shape[1])
    named = [routes[k : k + 1, :] == expert for k in range(2)]
    at = ranks(named[0] | named[1]) == slot.astype(F32)
    return [n & at for n in named]


def placed_packed(routes, regions):
    s = lax.broadcasted_iota(jnp.int32, (8 * regions, routes.shape[1]), 0)
    expert = s // 8
    named = [routes[k : k + 1, :] == expert for k in range(2)]
    rank = ranks(named[0] | named[1])
    main = rank == (s % 8).astype(F32)
    late = (rank == (8 + (s % 8) // 4).astype(F32)) & (s % 4 == 0)
    return [n & main for n in named], [n & late for n in named]


def pack_kernel(regions, tok, gain, grad, routes, out):
    at = placed(routes[...], regions)
    pick = (at[0] | at[1]).astype(F32).astype(BF)
    scaled = (tok[...].astype(F32) * gain[...]).astype(BF)
    rows = dot(pick, jnp.concatenate([scaled, grad[...]], axis=1)).astype(BF)
    cut = 8 * regions
    out[...] = encode(rows[:cut], rows[cut:], fold_matrix(regions))


def pack(tok, gain, grad, routes, regions):
    width = tok.shape[1]
    return pl.pallas_call(
        functools.partial(pack_kernel, regions),
        out_shape=jax.ShapeDtypeStruct((8 * regions, packed_lanes(width)), BF),
        compiler_params=params(),
    )(tok, gain, grad, routes)


def inverse(squares, full):
    return lax.rsqrt(jnp.sum(squares, axis=0, keepdims=True) / full + 1e-06)


def spread_kernel(regions, full, squares, routes, out):
    inv = inverse(squares[...], full)
    main, late = placed_packed(routes[...], regions)
    lane = lax.broadcasted_iota(jnp.int32, out.shape, 1)
    first = jnp.sum(jnp.where(main[0] | main[1], inv, 0.0), axis=1, keepdims=True)
    second = jnp.sum(jnp.where(late[0] | late[1], inv, 0.0), axis=1, keepdims=True)
    out[...] = jnp.where(lane == 0, first, jnp.where(lane == 1, second, 0.0))


def spread(squares, routes, regions, full):
    return pl.pallas_call(
        functools.partial(spread_kernel, regions, full),
        out_shape=jax.ShapeDtypeStruct((8 * regions, 128), F32),
        compiler_params=params(),
    )(squares, routes)


def hidden_kernel(regions, width, scales, block, gate_w, up_w, down_w, hid_out, gate_out, up_out, scal_out, acc_g, acc_u, acc_h):
    step = pl.program_id(0)
    fold = fold_matrix(regions)

    @pl.when(step == 0)
    def _():
        acc_g[...] = jnp.zeros_like(acc_g)
        acc_u[...] = jnp.zeros_like(acc_u)
        acc_h[...] = jnp.zeros_like(acc_h)

    rows_in, rows_grad = decode(block[0], width, fold)
    acc_g[...] += dot(rows_in, gate_w[0])
    acc_u[...] += dot(rows_in, up_w[0])
    acc_h[...] += dot(rows_grad, down_w[0], NT)

    @pl.when(step == pl.num_programs(0) - 1)
    def _():
        cut = 8 * regions
        i = lax.broadcasted_iota(jnp.int32, (2 * regions, cut), 0)
        j = lax.broadcasted_iota(jnp.int32, (2 * regions, cut), 1)
        low = dot((j == 4 * i).astype(F32), scales[...], precision=lax.Precision.HIGHEST)
        inv = jnp.concatenate([scales[:, 0:1], low[:, 1:2]], axis=0)
        gate_raw, up_raw, grad_hidden = acc_g[...], acc_u[...], acc_h[...]
        gate_pre, up_pre = gate_raw * inv, up_raw * inv
        sig = jax.nn.sigmoid(gate_pre)
        act = gate_pre * sig
        hidden = (act * up_pre).astype(BF)
        grad_gate = (grad_hidden * up_pre * sig * (1.0 + gate_pre * (1.0 - sig))).astype(BF)
        grad_up = (grad_hidden * act).astype(BF)
        hid_out[...] = hidden
        gate_out[...] = grad_gate
        up_out[...] = grad_up
        comb = jnp.sum(hidden.astype(F32) * grad_hidden, axis=1, keepdims=True)
        inner = jnp.sum(grad_gate.astype(F32) * gate_raw + grad_up.astype(F32) * up_raw, axis=1, keepdims=True)
        lane = lax.broadcasted_iota(jnp.int32, (cut, 128), 1)
        lane_low = lax.broadcasted_iota(jnp.int32, (2 * regions, 128), 1)
        main = jnp.where(lane == 0, comb[:cut], jnp.where(lane == 1, inner[:cut], 0.0))
        rest = jnp.where(lane_low == 2, comb[cut:], jnp.where(lane_low == 3, inner[cut:], 0.0))
        a = lax.broadcasted_iota(jnp.int32, (cut, 2 * regions), 0)
        b = lax.broadcasted_iota(jnp.int32, (cut, 2 * regions), 1)
        scal_out[...] = main + dot((a == 4 * b).astype(F32), rest, precision=lax.Precision.HIGHEST)


def hidden_part(scales, blocks, gate_w, up_w, down_w, regions):
    count, rows, lanes = blocks.shape
    width = gate_w.shape[1] // count
    units = gate_w.shape[2]
    total = 10 * regions
    whole = lambda shape: pl.BlockSpec(shape, lambda z: (0,) * len(shape))
    return pl.pallas_call(
        functools.partial(hidden_kernel, regions, width),
        grid=(count,),
        in_specs=[
            whole((rows, 128)),
            pl.BlockSpec((1, rows, lanes), lambda z: (z, 0, 0)),
            pl.BlockSpec((1, width, units), lambda z: (0, z, 0)),
            pl.BlockSpec((1, width, units), lambda z: (0, z, 0)),
            pl.BlockSpec((1, units, width), lambda z: (0, 0, z)),
        ],
        out_specs=[whole((total, units))] * 3 + [whole((rows, 128))],
        out_shape=[jax.ShapeDtypeStruct((total, units), BF)] * 3 + [jax.ShapeDtypeStruct((rows, 128), F32)],
        scratch_shapes=[pltpu.VMEM((total, units), F32)] * 3,
        compiler_params=params(),
    )(scales, blocks, gate_w, up_w, down_w)


def back_kernel(regions, hid, gate_g, up_g, gate_w, up_w, down_w, out):
    moe = dot(hid[...], down_w[0]).astype(BF)
    grad = (dot(gate_g[...], gate_w[0], NT) + dot(up_g[...], up_w[0], NT)).astype(BF)
    both = jnp.concatenate([moe, grad], axis=1)
    cut = 8 * regions
    out[0] = encode(both[:cut], both[cut:], fold_matrix(regions))


def back_part(hid, gate_g, up_g, gate_w, up_w, down_w, regions, count):
    width = gate_w.shape[1] // count
    units = gate_w.shape[2]
    total = 10 * regions
    lanes = packed_lanes(width)
    rows = 8 * regions
    whole = lambda shape: pl.BlockSpec(shape, lambda z: (0,) * len(shape))
    return pl.pallas_call(
        functools.partial(back_kernel, regions),
        grid=(count,),
        in_specs=[whole((total, units))] * 3
        + [
            pl.BlockSpec((1, width, units), lambda z: (0, z, 0)),
            pl.BlockSpec((1, width, units), lambda z: (0, z, 0)),
            pl.BlockSpec((1, units, width), lambda z: (0, 0, z)),
        ],
        out_specs=pl.BlockSpec((1, rows, lanes), lambda z: (z, 0, 0)),
        out_shape=jax.ShapeDtypeStruct((count, rows, lanes), BF),
        compiler_params=params(),
    )(hid, gate_g, up_g, gate_w, up_w, down_w)


def scalars_kernel(regions, scal, routes, weights, out):
    main, late = placed_packed(routes[...], regions)
    here = scal[...]
    parts = []
    inner = 0.0
    for k in range(2):
        comb = jnp.where(main[k], here[:, 0:1], 0.0) + jnp.where(late[k], here[:, 2:3], 0.0)
        part = jnp.where(main[k], here[:, 1:2], 0.0) + jnp.where(late[k], here[:, 3:4], 0.0)
        parts.append(jnp.sum(comb, axis=0, keepdims=True))
        inner = inner + weights[k : k + 1, :] * jnp.sum(part, axis=0, keepdims=True)
    row = lax.broadcasted_iota(jnp.int32, out.shape, 0)
    out[...] = jnp.where(row == 0, parts[0], jnp.where(row == 1, parts[1], jnp.where(row == 2, inner, 0.0)))


def scalars(scal, routes, weights, regions):
    return pl.pallas_call(
        functools.partial(scalars_kernel, regions),
        out_shape=jax.ShapeDtypeStruct((8, routes.shape[1]), F32),
        compiler_params=params(),
    )(scal, routes, weights)


def combine_rows(block, width, routes, weights, regions):
    at = placed(routes, regions)
    weight = jnp.where(at[0], weights[0:1, :], 0.0) + jnp.where(at[1], weights[1:2, :], 0.0)
    high = weight.astype(BF)
    low = (weight - high.astype(F32)).astype(BF)
    return [dot(high, rows, TN) + dot(low, rows, TN) for rows in decode(block, width, fold_matrix(regions))]


def final_kernel(regions, full, back, tok, gain, squares, sums, routes, weights, moe_out, grad_out, comb_out):
    width = tok.shape[1]
    moe, grad = combine_rows(back[...], width, routes[...], weights[...], regions)
    moe_out[...] = moe.astype(BF)
    total = jnp.sum(sums[...], axis=0)
    comb_out[...] = total[0:2]
    inv_row = inverse(squares[...], full)
    row = lax.broadcasted_iota(jnp.int32, total.shape, 0)
    columns = jnp.transpose(jnp.where(row == 3, inv_row, total))
    inner, inv = columns[:, 2:3], columns[:, 3:4]
    scaled = gain[...] * grad
    grad_out[...] = (inv * scaled - tok[...].astype(F32) * (inv * inv * inv * inner / full)).astype(BF)


def final(back, tok, gain, squares, sums, routes, weights, regions, full):
    count, width = tok.shape
    return pl.pallas_call(
        functools.partial(final_kernel, regions, full),
        out_shape=[
            jax.ShapeDtypeStruct((count, width), BF),
            jax.ShapeDtypeStruct((count, width), BF),
            jax.ShapeDtypeStruct((2, count), F32),
        ],
        compiler_params=params(),
    )(back, tok, gain, squares, sums, routes, weights)


def swap(array, regions):
    split = array.reshape(regions, 8, array.shape[1])
    moved = lax.all_to_all(split, "region", split_axis=0, concat_axis=0, tiled=True)
    return moved.reshape(array.shape)


def on_device(tokens, norm_gain, w_gate, w_up, w_down, routes, combine, grad_out):
    regions = lax.axis_size("region")
    depth = lax.axis_size("local")
    full = depth * tokens.shape[1]
    gain = norm_gain.reshape(1, -1)
    routes, weights = routes.T, combine.T
    wide = tokens.astype(F32)
    packed = pack(tokens, gain, grad_out, routes, regions)
    squares = lax.all_gather(jnp.sum(wide * wide, axis=1), "local")
    rows = swap(packed, regions)
    scales = swap(spread(squares, routes, regions, full), regions)
    blocks = lax.all_gather(rows, "local")
    hid, gate_g, up_g, scal = hidden_part(scales, blocks, w_gate, w_up, w_down, regions)
    sums = lax.all_gather(scalars(swap(scal, regions), routes, weights, regions), "local")
    partial = back_part(hid, gate_g, up_g, w_gate, w_up, w_down, regions, depth)
    summed = lax.psum_scatter(partial, "local", scatter_dimension=0)
    back = swap(summed, regions)
    moe, grad, comb = final(back, tokens, gain, squares, sums, routes, weights, regions, full)
    return moe, grad, comb.T


def solution(mesh):
    specs = (
        P("region", "local"),
        P("local"),
        P("region", None, "local"),
        P("region", None, "local"),
        P("region", "local", None),
        P("region", None),
        P("region", None),
        P("region", "local"),
    )
    return jax.shard_map(
        on_device,
        mesh=mesh,
        in_specs=specs,
        out_specs=(P("region", "local"), P("region", "local"), P("region", None)),
        check_vma=False,
    )
```

```python
import functools

import jax
import jax.numpy as jnp
from jax import lax
from jax.experimental import pallas as pl
from jax.experimental.pallas import tpu as pltpu
from jax.sharding import PartitionSpec as P

BF = jnp.bfloat16
F32 = jnp.float32
NT = (((1,), (1,)), ((), ()))
TN = (((0,), (0,)), ((), ()))
VMEM_LIMIT = 48 * 1024 * 1024
EARLY = 384


def fold_lanes(width):
    return 128 * -(-width // 256)


def packed_lanes(width):
    return 2 * width + fold_lanes(width)


def dot(a, b, dims=(((1,), (0,)), ((), ())), precision=None):
    return lax.dot_general(a, b, dims, precision=precision, preferred_element_type=F32)


def params(**kw):
    return pltpu.CompilerParams(vmem_limit_bytes=VMEM_LIMIT, **kw)


def fold_matrix(regions):
    rows = 8 * regions
    i = lax.broadcasted_iota(jnp.int32, (rows, rows), 0)
    j = lax.broadcasted_iota(jnp.int32, (rows, rows), 1)
    return (j == 4 * (i % (2 * regions)) + i // (2 * regions)).astype(BF)


def encode(main, rest, fold):
    width = main.shape[1] // 2
    lanes = fold_lanes(width)
    pad = 2 * lanes - width
    parts = []
    for side in range(2):
        parts.append(rest[:, side * width : side * width + lanes])
        tail = rest[:, side * width + lanes : (side + 1) * width]
        if pad:
            tail = jnp.concatenate([tail, jnp.zeros((rest.shape[0], pad), rest.dtype)], axis=1)
        parts.append(tail)
    stacked = jnp.concatenate(parts, axis=0)
    return jnp.concatenate([main, dot(fold, stacked, TN).astype(BF)], axis=1)


def decode(block, width, fold):
    lanes = fold_lanes(width)
    rows = block.shape[0]
    rest = dot(fold, block[:, 2 * width :]).astype(BF)
    few = rows // 4
    sides = []
    for side in range(2):
        head = rest[(2 * side) * few : (2 * side + 1) * few]
        tail = rest[(2 * side + 1) * few : (2 * side + 2) * few, : width - lanes]
        low = jnp.concatenate([head, tail], axis=1)
        sides.append(jnp.concatenate([block[:, side * width : (side + 1) * width], low], axis=0))
    return sides


def slot_ids(regions, tokens):
    s = lax.broadcasted_iota(jnp.int32, (10 * regions, tokens), 0)
    late = s - 8 * regions
    expert = jnp.where(late < 0, s // 8, late // 2)
    slot = jnp.where(late < 0, s % 8, 8 + late % 2)
    return expert, slot


def ranks(named):
    count = named.shape[1]
    before = lax.broadcasted_iota(jnp.int32, (count, count), 0)
    after = lax.broadcasted_iota(jnp.int32, (count, count), 1)
    return dot(named.astype(F32).astype(BF), (before < after).astype(F32).astype(BF))


def placed(routes, regions):
    expert, slot = slot_ids(regions, routes.shape[1])
    named = [routes[k : k + 1, :] == expert for k in range(2)]
    at = ranks(named[0] | named[1]) == slot.astype(F32)
    return [n & at for n in named]


def placed_packed(routes, regions):
    s = lax.broadcasted_iota(jnp.int32, (8 * regions, routes.shape[1]), 0)
    expert = s // 8
    named = [routes[k : k + 1, :] == expert for k in range(2)]
    rank = ranks(named[0] | named[1])
    main = rank == (s % 8).astype(F32)
    late = (rank == (8 + (s % 8) // 4).astype(F32)) & (s % 4 == 0)
    return [n & main for n in named], [n & late for n in named]


def fold_part(regions, part):
    i = lax.broadcasted_iota(jnp.int32, (2 * regions, 8 * regions), 0)
    j = lax.broadcasted_iota(jnp.int32, (2 * regions, 8 * regions), 1)
    return (j == 4 * i + part).astype(F32).astype(BF)


def pack_kernel(regions, tok, gain, grad, routes, out, early):
    at = placed(routes[...], regions)
    pick = (at[0] | at[1]).astype(F32).astype(BF)
    late = out.shape[1] * 2 // 5
    scaled = (tok[...].astype(F32) * gain[...]).astype(BF)
    rows = dot(pick, jnp.concatenate([scaled[:, :late], grad[:, :late]], axis=1)).astype(BF)
    cut = 8 * regions
    out[...] = encode(rows[:cut], rows[cut:], fold_matrix(regions))
    early[...] = jnp.concatenate([scaled[:, late:], grad[:, late:]], axis=1)


def pack(tok, gain, grad, routes, regions):
    count, width = tok.shape
    return pl.pallas_call(
        functools.partial(pack_kernel, regions),
        out_shape=[
            jax.ShapeDtypeStruct((8 * regions, packed_lanes(width - EARLY)), BF),
            jax.ShapeDtypeStruct((count, 2 * EARLY), BF),
        ],
        compiler_params=params(),
    )(tok, gain, grad, routes)


def pack_early_kernel(regions, early, routes, out):
    depth, _, lanes = early.shape
    at = placed(routes[...], regions)
    pick = (at[0] | at[1]).astype(F32).astype(BF)
    cut = 8 * regions
    rests = []
    for z in range(depth):
        rows = dot(pick, early[z]).astype(BF)
        out[:, z * lanes : (z + 1) * lanes] = rows[:cut]
        rests.append(rows[cut:])
    for half in range(depth // 4):
        stacked = jnp.concatenate([rests[part * (depth // 4) + half] for part in range(4)], axis=0)
        at_lane = (depth + half) * lanes
        out[:, at_lane : at_lane + lanes] = dot(fold_matrix(regions), stacked, TN).astype(BF)


def pack_early(early, routes, regions):
    depth, _, lanes = early.shape
    return pl.pallas_call(
        functools.partial(pack_early_kernel, regions),
        out_shape=jax.ShapeDtypeStruct((8 * regions, lanes * depth * 5 // 4), BF),
        compiler_params=params(),
    )(early, routes)


def inverse(squares, full):
    return lax.rsqrt(squares / full + 1e-06)


def spread_kernel(regions, full, squares, routes, out):
    inv = inverse(squares[...], full)
    main, late = placed_packed(routes[...], regions)
    lane = lax.broadcasted_iota(jnp.int32, out.shape, 1)
    first = jnp.sum(jnp.where(main[0] | main[1], inv, 0.0), axis=1, keepdims=True)
    second = jnp.sum(jnp.where(late[0] | late[1], inv, 0.0), axis=1, keepdims=True)
    out[...] = jnp.where(lane == 0, first, jnp.where(lane == 1, second, 0.0))


def spread(squares, routes, regions, full):
    return pl.pallas_call(
        functools.partial(spread_kernel, regions, full),
        out_shape=jax.ShapeDtypeStruct((8 * regions, 128), F32),
        compiler_params=params(),
    )(squares, routes)


def early_kernel(regions, main, rest, gate_w, up_w, down_w, acc_g, acc_u, acc_h):
    step = pl.program_id(0)
    lanes = main.shape[1]
    width = lanes // 2
    skip = gate_w.shape[1] - width

    @pl.when(step == 0)
    def _():
        acc_g[...] = jnp.zeros_like(acc_g)
        acc_u[...] = jnp.zeros_like(acc_u)
        acc_h[...] = jnp.zeros_like(acc_h)

    part = step // (pl.num_programs(0) // 4)
    low = dot(fold_part(regions, part), rest[...]).astype(BF)
    rows = jnp.concatenate([main[...], low], axis=0)
    acc_g[...] += dot(rows[:, :width], gate_w[0, skip:, :])
    acc_u[...] += dot(rows[:, :width], up_w[0, skip:, :])
    acc_h[...] += dot(rows[:, width:], down_w[0, :, skip:], NT)


def whole(shape):
    return pl.BlockSpec(shape, lambda z: (0,) * len(shape))


def weight_specs(width, units):
    return [
        pl.BlockSpec((1, width, units), lambda z: (0, z, 0)),
        pl.BlockSpec((1, width, units), lambda z: (0, z, 0)),
        pl.BlockSpec((1, units, width), lambda z: (0, 0, z)),
    ]


def early_part(rows, gate_w, up_w, down_w, regions, depth):
    cut = rows.shape[0]
    width, units = gate_w.shape[1] // depth, gate_w.shape[2]
    lanes = 2 * EARLY
    total = 10 * regions
    return pl.pallas_call(
        functools.partial(early_kernel, regions),
        grid=(depth,),
        in_specs=[
            pl.BlockSpec((cut, lanes), lambda z: (0, z)),
            pl.BlockSpec((cut, lanes), lambda z: (0, depth + z % (depth // 4))),
        ]
        + weight_specs(width, units),
        out_specs=[whole((total, units))] * 3,
        out_shape=[jax.ShapeDtypeStruct((total, units), F32)] * 3,
        compiler_params=params(),
    )(rows, rows, gate_w, up_w, down_w)


def hidden_kernel(
    regions, width, scales, block, gate_w, up_w, down_w, pre_g, pre_u, pre_h, hid_out, gate_out, up_out, scal_out, acc_g, acc_u, acc_h
):
    step = pl.program_id(0)
    fold = fold_matrix(regions)

    @pl.when(step == 0)
    def _():
        acc_g[...] = pre_g[...]
        acc_u[...] = pre_u[...]
        acc_h[...] = pre_h[...]

    rows_in, rows_grad = decode(block[0], width, fold)
    acc_g[...] += dot(rows_in, gate_w[0, :width, :])
    acc_u[...] += dot(rows_in, up_w[0, :width, :])
    acc_h[...] += dot(rows_grad, down_w[0, :, :width], NT)

    @pl.when(step == pl.num_programs(0) - 1)
    def _():
        cut = 8 * regions
        i = lax.broadcasted_iota(jnp.int32, (2 * regions, cut), 0)
        j = lax.broadcasted_iota(jnp.int32, (2 * regions, cut), 1)
        low = dot((j == 4 * i).astype(F32), scales[...], precision=lax.Precision.HIGHEST)
        inv = jnp.concatenate([scales[:, 0:1], low[:, 1:2]], axis=0)
        gate_raw, up_raw, grad_hidden = acc_g[...], acc_u[...], acc_h[...]
        gate_pre, up_pre = gate_raw * inv, up_raw * inv
        sig = jax.nn.sigmoid(gate_pre)
        act = gate_pre * sig
        hidden = (act * up_pre).astype(BF)
        grad_gate = (grad_hidden * up_pre * sig * (1.0 + gate_pre * (1.0 - sig))).astype(BF)
        grad_up = (grad_hidden * act).astype(BF)
        hid_out[...] = hidden
        gate_out[...] = grad_gate
        up_out[...] = grad_up
        comb = jnp.sum(hidden.astype(F32) * grad_hidden, axis=1, keepdims=True)
        inner = jnp.sum(grad_gate.astype(F32) * gate_raw + grad_up.astype(F32) * up_raw, axis=1, keepdims=True)
        lane = lax.broadcasted_iota(jnp.int32, (cut, 128), 1)
        lane_low = lax.broadcasted_iota(jnp.int32, (2 * regions, 128), 1)
        main = jnp.where(lane == 0, comb[:cut], jnp.where(lane == 1, inner[:cut], 0.0))
        rest = jnp.where(lane_low == 2, comb[cut:], jnp.where(lane_low == 3, inner[cut:], 0.0))
        a = lax.broadcasted_iota(jnp.int32, (cut, 2 * regions), 0)
        b = lax.broadcasted_iota(jnp.int32, (cut, 2 * regions), 1)
        scal_out[...] = main + dot((a == 4 * b).astype(F32), rest, precision=lax.Precision.HIGHEST)


def hidden_part(scales, blocks, gate_w, up_w, down_w, sums, regions):
    depth, rows, lanes = blocks.shape
    width, units = gate_w.shape[1] // depth, gate_w.shape[2]
    total = 10 * regions
    return pl.pallas_call(
        functools.partial(hidden_kernel, regions, width - EARLY),
        grid=(depth,),
        in_specs=[whole((rows, 128)), pl.BlockSpec((1, rows, lanes), lambda z: (z, 0, 0))]
        + weight_specs(width, units)
        + [whole((total, units))] * 3,
        out_specs=[whole((total, units))] * 3 + [whole((rows, 128))],
        out_shape=[jax.ShapeDtypeStruct((total, units), BF)] * 3 + [jax.ShapeDtypeStruct((rows, 128), F32)],
        scratch_shapes=[pltpu.VMEM((total, units), F32)] * 3,
        compiler_params=params(),
    )(scales, blocks, gate_w, up_w, down_w, *sums)


def back_early_kernel(regions, hid, gate_g, up_g, gate_w, up_w, down_w, out):
    depth = pl.num_programs(0)
    step = pl.program_id(0)
    skip = gate_w.shape[1] - EARLY
    lanes = 2 * EARLY
    moe = dot(hid[...], down_w[0, :, skip:]).astype(BF)
    grad = (dot(gate_g[...], gate_w[0, skip:, :], NT) + dot(up_g[...], up_w[0, skip:, :], NT)).astype(BF)
    both = jnp.concatenate([moe, grad], axis=1)
    cut = 8 * regions
    quarter = depth // 4
    out[:, pl.ds(pl.multiple_of(step * lanes, 128), lanes)] = both[:cut]
    spot = pl.ds(pl.multiple_of((depth + step % quarter) * lanes, 128), lanes)
    low = dot(fold_part(regions, step // quarter), both[cut:], TN).astype(BF)

    @pl.when(step < quarter)
    def _():
        out[:, spot] = low

    @pl.when(step >= quarter)
    def _():
        out[:, spot] = out[:, spot] + low


def back_early(hid, gate_g, up_g, gate_w, up_w, down_w, regions, depth):
    width, units = gate_w.shape[1] // depth, gate_w.shape[2]
    total = 10 * regions
    shape = (8 * regions, 2 * EARLY * depth * 5 // 4)
    return pl.pallas_call(
        functools.partial(back_early_kernel, regions),
        grid=(depth,),
        in_specs=[whole((total, units))] * 3 + weight_specs(width, units),
        out_specs=whole(shape),
        out_shape=jax.ShapeDtypeStruct(shape, BF),
        compiler_params=params(),
    )(hid, gate_g, up_g, gate_w, up_w, down_w)


def back_kernel(regions, hid, gate_g, up_g, gate_w, up_w, down_w, out):
    late = gate_w.shape[1] - EARLY
    moe = dot(hid[...], down_w[0, :, :late]).astype(BF)
    grad = (dot(gate_g[...], gate_w[0, :late, :], NT) + dot(up_g[...], up_w[0, :late, :], NT)).astype(BF)
    both = jnp.concatenate([moe, grad], axis=1)
    cut = 8 * regions
    out[0] = encode(both[:cut], both[cut:], fold_matrix(regions))


def back_part(hid, gate_g, up_g, gate_w, up_w, down_w, regions, depth):
    width, units = gate_w.shape[1] // depth, gate_w.shape[2]
    total = 10 * regions
    lanes = packed_lanes(width - EARLY)
    rows = 8 * regions
    return pl.pallas_call(
        functools.partial(back_kernel, regions),
        grid=(depth,),
        in_specs=[whole((total, units))] * 3 + weight_specs(width, units),
        out_specs=pl.BlockSpec((1, rows, lanes), lambda z: (z, 0, 0)),
        out_shape=jax.ShapeDtypeStruct((depth, rows, lanes), BF),
        compiler_params=params(),
    )(hid, gate_g, up_g, gate_w, up_w, down_w)


def scalars_kernel(regions, scal, routes, weights, out):
    main, late = placed_packed(routes[...], regions)
    here = scal[...]
    parts = []
    inner = 0.0
    for k in range(2):
        comb = jnp.where(main[k], here[:, 0:1], 0.0) + jnp.where(late[k], here[:, 2:3], 0.0)
        part = jnp.where(main[k], here[:, 1:2], 0.0) + jnp.where(late[k], here[:, 3:4], 0.0)
        parts.append(jnp.sum(comb, axis=0, keepdims=True))
        inner = inner + weights[k : k + 1, :] * jnp.sum(part, axis=0, keepdims=True)
    row = lax.broadcasted_iota(jnp.int32, out.shape, 0)
    out[...] = jnp.where(row == 0, parts[0], jnp.where(row == 1, parts[1], jnp.where(row == 2, inner, 0.0)))


def scalars(scal, routes, weights, regions):
    return pl.pallas_call(
        functools.partial(scalars_kernel, regions),
        out_shape=jax.ShapeDtypeStruct((8, routes.shape[1]), F32),
        compiler_params=params(),
    )(scal, routes, weights)


def combining(routes, weights, regions):
    at = placed(routes, regions)
    weight = jnp.where(at[0], weights[0:1, :], 0.0) + jnp.where(at[1], weights[1:2, :], 0.0)
    high = weight.astype(BF)
    return high, (weight - high.astype(F32)).astype(BF)


def combine_early_kernel(regions, back, routes, weights, out):
    depth, _, lanes = out.shape
    high, low = combining(routes[...], weights[...], regions)
    quarter = depth // 4
    rests = [dot(fold_matrix(regions), back[:, (depth + half) * lanes : (depth + half + 1) * lanes]).astype(BF) for half in range(quarter)]
    few = 2 * regions
    for z in range(depth):
        part = z // quarter
        rest = rests[z % quarter][part * few : (part + 1) * few]
        rows = jnp.concatenate([back[:, z * lanes : (z + 1) * lanes], rest], axis=0)
        out[z] = (dot(high, rows, TN) + dot(low, rows, TN)).astype(BF)


def combine_early(back, routes, weights, regions, depth):
    return pl.pallas_call(
        functools.partial(combine_early_kernel, regions),
        out_shape=jax.ShapeDtypeStruct((depth, routes.shape[1], 2 * EARLY), BF),
        compiler_params=params(),
    )(back, routes, weights)


def final_kernel(regions, full, back, early, tok, gain, squares, sums, routes, weights, moe_out, grad_out, comb_out):
    late = tok.shape[1] - EARLY
    high, low = combining(routes[...], weights[...], regions)
    moe, grad = [dot(high, rows, TN) + dot(low, rows, TN) for rows in decode(back[...], late, fold_matrix(regions))]
    moe_out[:, :late] = moe.astype(BF)
    moe_out[:, late:] = early[:, :EARLY]
    total = sums[...]
    comb_out[...] = total[0:2]
    row = lax.broadcasted_iota(jnp.int32, total.shape, 0)
    columns = jnp.transpose(jnp.where(row == 3, inverse(squares[...], full), total))
    inner, inv = columns[:, 2:3], columns[:, 3:4]
    scaled = gain[...] * jnp.concatenate([grad, early[:, EARLY:].astype(F32)], axis=1)
    grad_out[...] = (inv * scaled - tok[...].astype(F32) * (inv * inv * inv * inner / full)).astype(BF)


def final(back, early, tok, gain, squares, sums, routes, weights, regions, full):
    count, width = tok.shape
    return pl.pallas_call(
        functools.partial(final_kernel, regions, full),
        out_shape=[
            jax.ShapeDtypeStruct((count, width), BF),
            jax.ShapeDtypeStruct((count, width), BF),
            jax.ShapeDtypeStruct((2, count), F32),
        ],
        compiler_params=params(),
    )(back, early, tok, gain, squares, sums, routes, weights)


def swap(array, regions):
    split = array.reshape(regions, 8, array.shape[1])
    moved = lax.all_to_all(split, "region", split_axis=0, concat_axis=0, tiled=True)
    return moved.reshape(array.shape)


def add_over_local(array):
    depth = lax.axis_size("local")
    step = 1
    while step < depth:
        array = array + lax.ppermute(array, "local", [(z, z ^ step) for z in range(depth)])
        step *= 2
    return array


def on_device(tokens, norm_gain, w_gate, w_up, w_down, routes, combine, grad_out):
    regions = lax.axis_size("region")
    depth = lax.axis_size("local")
    full = depth * tokens.shape[1]
    gain = norm_gain.reshape(1, -1)
    routes, weights = routes.T, combine.T
    wide = tokens.astype(F32)
    packed, early = pack(tokens, gain, grad_out, routes, regions)
    early = lax.all_gather(early, "local")
    squares = add_over_local(jnp.sum(wide * wide, axis=1).reshape(1, -1))
    blocks = lax.all_gather(swap(packed, regions), "local")
    scales = swap(spread(squares, routes, regions, full), regions)
    rows = swap(pack_early(early, routes, regions), regions)
    sums = early_part(rows, w_gate, w_up, w_down, regions, depth)
    hid, gate_g, up_g, scal = hidden_part(scales, blocks, w_gate, w_up, w_down, sums, regions)
    inner = (hid, gate_g, up_g, w_gate, w_up, w_down, regions, depth)
    back_rows = back_early(*inner)
    partial = back_part(*inner)
    sums = add_over_local(scalars(swap(scal, regions), routes, weights, regions))
    summed = lax.psum_scatter(partial, "local", scatter_dimension=0)
    shares = combine_early(swap(back_rows, regions), routes, weights, regions, depth)
    own = lax.psum_scatter(shares, "local", scatter_dimension=0)
    moe, grad, comb = final(swap(summed, regions), own, tokens, gain, squares, sums, routes, weights, regions, full)
    return moe, grad, comb.T


def solution(mesh):
    specs = (
        P("region", "local"),
        P("local"),
        P("region", None, "local"),
        P("region", None, "local"),
        P("region", "local", None),
        P("region", None),
        P("region", None),
        P("region", "local"),
    )
    return jax.shard_map(
        on_device,
        mesh=mesh,
        in_specs=specs,
        out_specs=(P("region", "local"), P("region", "local"), P("region", None)),
        check_vma=False,
    )
```

```python
import functools

import jax
import jax.numpy as jnp
from jax import lax
from jax.experimental import pallas as pl
from jax.experimental.pallas import tpu as pltpu
from jax.sharding import PartitionSpec as P

BF = jnp.bfloat16
F32 = jnp.float32
NT = (((1,), (1,)), ((), ()))
TN = (((0,), (0,)), ((), ()))
VMEM_LIMIT = 48 * 1024 * 1024
EARLY = 384


def fold_lanes(width):
    return 128 * -(-width // 256)


def packed_lanes(width):
    return 2 * width + fold_lanes(width)


def dot(a, b, dims=(((1,), (0,)), ((), ())), precision=None):
    return lax.dot_general(a, b, dims, precision=precision, preferred_element_type=F32)


def params(**kw):
    return pltpu.CompilerParams(vmem_limit_bytes=VMEM_LIMIT, **kw)


def whole(shape):
    return pl.BlockSpec(shape, lambda *_: (0,) * len(shape))


def fold_matrix(regions):
    rows = 8 * regions
    i = lax.broadcasted_iota(jnp.int32, (rows, rows), 0)
    j = lax.broadcasted_iota(jnp.int32, (rows, rows), 1)
    return (j == 4 * (i % (2 * regions)) + i // (2 * regions)).astype(BF)


def encode(main, rest, fold):
    width = main.shape[1] // 2
    lanes = fold_lanes(width)
    pad = 2 * lanes - width
    parts = []
    for side in range(2):
        parts.append(rest[:, side * width : side * width + lanes])
        tail = rest[:, side * width + lanes : (side + 1) * width]
        if pad:
            tail = jnp.concatenate([tail, jnp.zeros((rest.shape[0], pad), rest.dtype)], axis=1)
        parts.append(tail)
    stacked = jnp.concatenate(parts, axis=0)
    return jnp.concatenate([main, dot(fold, stacked, TN).astype(BF)], axis=1)


def decode(block, width, fold):
    lanes = fold_lanes(width)
    rows = block.shape[0]
    rest = dot(fold, block[:, 2 * width :]).astype(BF)
    few = rows // 4
    sides = []
    for side in range(2):
        head = rest[(2 * side) * few : (2 * side + 1) * few]
        tail = rest[(2 * side + 1) * few : (2 * side + 2) * few, : width - lanes]
        low = jnp.concatenate([head, tail], axis=1)
        sides.append(jnp.concatenate([block[:, side * width : (side + 1) * width], low], axis=0))
    return sides


def slot_ids(regions, tokens):
    s = lax.broadcasted_iota(jnp.int32, (10 * regions, tokens), 0)
    late = s - 8 * regions
    expert = jnp.where(late < 0, s // 8, late // 2)
    slot = jnp.where(late < 0, s % 8, 8 + late % 2)
    return expert, slot


def ranks(named):
    count = named.shape[1]
    before = lax.broadcasted_iota(jnp.int32, (count, count), 0)
    after = lax.broadcasted_iota(jnp.int32, (count, count), 1)
    return dot(named.astype(F32).astype(BF), (before < after).astype(F32).astype(BF))


def placed(routes, regions):
    expert, slot = slot_ids(regions, routes.shape[1])
    named = [routes[k : k + 1, :] == expert for k in range(2)]
    at = ranks(named[0] | named[1]) == slot.astype(F32)
    return [n & at for n in named]


def placed_packed(routes, regions):
    s = lax.broadcasted_iota(jnp.int32, (8 * regions, routes.shape[1]), 0)
    expert = s // 8
    named = [routes[k : k + 1, :] == expert for k in range(2)]
    rank = ranks(named[0] | named[1])
    main = rank == (s % 8).astype(F32)
    late = (rank == (8 + (s % 8) // 4).astype(F32)) & (s % 4 == 0)
    return [n & main for n in named], [n & late for n in named]


def pack_kernel(regions, tok, gain, grad, routes, out, early):
    at = placed(routes[...], regions)
    pick = (at[0] | at[1]).astype(F32).astype(BF)
    late = out.shape[1] * 2 // 5
    scaled = (tok[...].astype(F32) * gain[...]).astype(BF)
    rows = dot(pick, jnp.concatenate([scaled[:, :late], grad[:, :late]], axis=1)).astype(BF)
    cut = 8 * regions
    out[...] = encode(rows[:cut], rows[cut:], fold_matrix(regions))
    early[...] = jnp.concatenate([scaled[:, late:], grad[:, late:]], axis=1)


def pack(tok, gain, grad, routes, regions):
    count, width = tok.shape
    shapes = [
        jax.ShapeDtypeStruct((8 * regions, packed_lanes(width - EARLY)), BF),
        jax.ShapeDtypeStruct((count, 2 * EARLY), BF),
    ]
    return once(functools.partial(pack_kernel, regions), shapes, tok, gain, grad, routes)


def inverse(squares, full):
    return lax.rsqrt(squares / full + 1e-06)


def triple(value):
    high = value.astype(BF)
    value = value - high.astype(F32)
    middle = value.astype(BF)
    return [high, middle, (value - middle.astype(F32)).astype(BF)]


def in_lanes(columns, rows):
    lane = lax.broadcasted_iota(jnp.int32, (rows, 128), 1)
    out = jnp.zeros((rows, 128), F32)
    for at, column in enumerate(columns):
        if column is not None:
            out = jnp.where(lane == at, column.astype(F32), out)
    return out.astype(BF)


def from_lanes(block, at):
    block = block.astype(F32)
    return block[:, at : at + 1] + block[:, at + 1 : at + 2] + block[:, at + 2 : at + 3]


def pack_early_kernel(regions, depth, full, routes, squares, *refs):
    blocks, out = refs[:-1], refs[-1]
    lanes = blocks[0].shape[1]
    early = {0: blocks[0][...]}
    half = depth // 2
    for hop in range(1, half):
        early[depth - hop] = blocks[2 * hop - 1][...]
        early[hop] = blocks[2 * hop][...]
    early[half] = jnp.concatenate([blocks[-2][...], blocks[-1][...]], axis=0)
    at = placed(routes[...], regions)
    pick = (at[0] | at[1]).astype(F32).astype(BF)
    cut = 8 * regions
    rests = []
    for z in range(depth):
        rows = dot(pick, early[z]).astype(BF)
        out[:, z * lanes : (z + 1) * lanes] = rows[:cut]
        rests.append(rows[cut:])
    for half in range(depth // 4):
        stacked = jnp.concatenate([rests[part * (depth // 4) + half] for part in range(4)], axis=0)
        at_lane = (depth + half) * lanes
        out[:, at_lane : at_lane + lanes] = dot(fold_matrix(regions), stacked, TN).astype(BF)
    inv = inverse(squares[...], full)
    columns = []
    for found in placed_packed(routes[...], regions):
        columns += triple(jnp.sum(jnp.where(found[0] | found[1], inv, 0.0), axis=1, keepdims=True))
    out[:, -128:] = in_lanes(columns, cut)


def once(kernel, out_shape, *operands):
    many = isinstance(out_shape, list)
    specs = [whole(shape.shape) for shape in (out_shape if many else [out_shape])]
    return pl.pallas_call(
        kernel,
        grid=(1,),
        in_specs=[whole(operand.shape) for operand in operands],
        out_specs=specs if many else specs[0],
        out_shape=out_shape,
        compiler_params=params(),
    )(*operands)


def early_shape(regions, depth):
    return (8 * regions, 2 * EARLY * depth * 5 // 4 + 128)


def pack_early(blocks, squares, routes, regions, depth, full):
    shape = jax.ShapeDtypeStruct(early_shape(regions, depth), BF)
    return once(functools.partial(pack_early_kernel, regions, depth, full), shape, routes, squares, *blocks)


def relative_specs(width, units, depth):
    return [
        pl.BlockSpec((1, width, units), lambda z, me: (0, (z + me[0]) % depth, 0)),
        pl.BlockSpec((1, width, units), lambda z, me: (0, (z + me[0]) % depth, 0)),
        pl.BlockSpec((1, units, width), lambda z, me: (0, 0, (z + me[0]) % depth)),
    ]


def hidden_kernel(
    regions, me, scales, block, main, rest, gate_w, up_w, down_w, hid_out, gate_out, up_out, scal_out, acc_g, acc_u, acc_h, fold
):
    step = pl.program_id(0)
    width = gate_w.shape[1]
    few = 2 * regions
    quarter = pl.num_programs(0) // 4

    @pl.when(step == 0)
    def _():
        fold[...] = fold_matrix(regions)
        acc_g[...] = jnp.zeros_like(acc_g)
        acc_u[...] = jnp.zeros_like(acc_u)
        acc_h[...] = jnp.zeros_like(acc_h)

    late_in, late_grad = decode(block[0], width - EARLY, fold[...])
    pick = fold[pl.ds(pl.multiple_of((step // quarter) * few, few), few), :]
    early = jnp.concatenate([main[...], dot(pick, rest[...]).astype(BF)], axis=0)
    rows_in = jnp.concatenate([late_in, early[:, :EARLY]], axis=1)
    rows_grad = jnp.concatenate([late_grad, early[:, EARLY:]], axis=1)
    acc_g[...] += dot(rows_in, gate_w[0])
    acc_u[...] += dot(rows_in, up_w[0])
    acc_h[...] += dot(rows_grad, down_w[0], NT)

    @pl.when(step == pl.num_programs(0) - 1)
    def _():
        cut = 8 * regions
        first = fold[0:few, :]
        inv = jnp.concatenate([from_lanes(scales[...], 0), from_lanes(dot(first, scales[...]), 3)], axis=0)
        gate_raw, up_raw, grad_hidden = acc_g[...], acc_u[...], acc_h[...]
        gate_pre, up_pre = gate_raw * inv, up_raw * inv
        sig = jax.nn.sigmoid(gate_pre)
        act = gate_pre * sig
        hidden = (act * up_pre).astype(BF)
        grad_gate = (grad_hidden * up_pre * sig * (1.0 + gate_pre * (1.0 - sig))).astype(BF)
        grad_up = (grad_hidden * act).astype(BF)
        hid_out[...] = hidden
        gate_out[...] = grad_gate
        up_out[...] = grad_up
        comb = jnp.sum(hidden.astype(F32) * grad_hidden, axis=1, keepdims=True)
        inner = jnp.sum(grad_gate.astype(F32) * gate_raw + grad_up.astype(F32) * up_raw, axis=1, keepdims=True)
        here = in_lanes(triple(comb[:cut]) + triple(inner[:cut]), cut)
        there = in_lanes([None] * 6 + triple(comb[cut:]) + triple(inner[cut:]), few)
        scal_out[...] = here + dot(first, there, TN).astype(BF)


def hidden_part(me, blocks, rows, gate_w, up_w, down_w, regions):
    depth, cut, lanes = blocks.shape
    width, units = gate_w.shape[1] // depth, gate_w.shape[2]
    total = 10 * regions
    return pl.pallas_call(
        functools.partial(hidden_kernel, regions),
        grid_spec=pltpu.PrefetchScalarGridSpec(
            num_scalar_prefetch=1,
            grid=(depth,),
            in_specs=[
                pl.BlockSpec((cut, 128), lambda z, me: (0, 2 * EARLY * depth * 5 // 512)),
                pl.BlockSpec((1, cut, lanes), lambda z, me: ((z + me[0]) % depth, 0, 0)),
                pl.BlockSpec((cut, 2 * EARLY), lambda z, me: (0, z)),
                pl.BlockSpec((cut, 2 * EARLY), lambda z, me: (0, depth + z % (depth // 4))),
            ]
            + relative_specs(width, units, depth),
            out_specs=[whole((total, units))] * 3 + [whole((cut, 128))],
            scratch_shapes=[pltpu.VMEM((total, units), F32)] * 3 + [pltpu.VMEM((cut, cut), BF)],
        ),
        out_shape=[jax.ShapeDtypeStruct((total, units), BF)] * 3 + [jax.ShapeDtypeStruct((cut, 128), BF)],
        compiler_params=params(),
    )(me, rows, blocks, rows, rows, gate_w, up_w, down_w)


def back_kernel(regions, me, hid, gate_g, up_g, scal, gate_w, up_w, down_w, late_out, early_out, fold):
    depth = pl.num_programs(0)
    step = pl.program_id(0)
    late = gate_w.shape[1] - EARLY
    lanes = 2 * EARLY
    few = 2 * regions
    cut = 8 * regions
    quarter = depth // 4

    @pl.when(step == 0)
    def _():
        fold[...] = fold_matrix(regions)
        early_out[:, -128:] = scal[...]

    moe = dot(hid[...], down_w[0]).astype(BF)
    grad = (dot(gate_g[...], gate_w[0], NT) + dot(up_g[...], up_w[0], NT)).astype(BF)
    both = jnp.concatenate([moe[:, :late], grad[:, :late]], axis=1)
    late_out[0] = encode(both[:cut], both[cut:], fold[...])
    both = jnp.concatenate([moe[:, late:], grad[:, late:]], axis=1)
    early_out[:, pl.ds(pl.multiple_of(step * lanes, 128), lanes)] = both[:cut]
    spot = pl.ds(pl.multiple_of((depth + step % quarter) * lanes, 128), lanes)
    pick = fold[pl.ds(pl.multiple_of((step // quarter) * few, few), few), :]
    low = dot(pick, both[cut:], TN).astype(BF)

    @pl.when(step < quarter)
    def _():
        early_out[:, spot] = low

    @pl.when(step >= quarter)
    def _():
        early_out[:, spot] = early_out[:, spot] + low


def back_part(me, hid, gate_g, up_g, scal, gate_w, up_w, down_w, regions, depth):
    width, units = gate_w.shape[1] // depth, gate_w.shape[2]
    total = 10 * regions
    cut = 8 * regions
    lanes = packed_lanes(width - EARLY)
    shape = early_shape(regions, depth)
    return pl.pallas_call(
        functools.partial(back_kernel, regions),
        grid_spec=pltpu.PrefetchScalarGridSpec(
            num_scalar_prefetch=1,
            grid=(depth,),
            in_specs=[whole((total, units))] * 3 + [whole((cut, 128))] + relative_specs(width, units, depth),
            out_specs=[pl.BlockSpec((1, cut, lanes), lambda z, me: ((z + me[0]) % depth, 0, 0)), whole(shape)],
            scratch_shapes=[pltpu.VMEM((cut, cut), BF)],
        ),
        out_shape=[jax.ShapeDtypeStruct((depth, cut, lanes), BF), jax.ShapeDtypeStruct(shape, BF)],
        compiler_params=params(),
    )(me, hid, gate_g, up_g, scal, gate_w, up_w, down_w)


def scalars(here, routes, weights, regions):
    main, late = placed_packed(routes, regions)
    parts = []
    inner = 0.0
    for k in range(2):
        comb = jnp.where(main[k], from_lanes(here, 0), 0.0) + jnp.where(late[k], from_lanes(here, 6), 0.0)
        part = jnp.where(main[k], from_lanes(here, 3), 0.0) + jnp.where(late[k], from_lanes(here, 9), 0.0)
        parts.append(jnp.sum(comb, axis=0, keepdims=True))
        inner = inner + weights[k : k + 1, :] * jnp.sum(part, axis=0, keepdims=True)
    row = lax.broadcasted_iota(jnp.int32, (8, routes.shape[1]), 0)
    return jnp.where(row == 0, parts[0], jnp.where(row == 1, parts[1], jnp.where(row == 2, inner, 0.0)))


def combining(routes, weights, regions):
    at = placed(routes, regions)
    weight = jnp.where(at[0], weights[0:1, :], 0.0) + jnp.where(at[1], weights[1:2, :], 0.0)
    high = weight.astype(BF)
    return high, (weight - high.astype(F32)).astype(BF)


def combine_early_kernel(regions, back, routes, weights, out, scal_out):
    scal_out[...] = scalars(back[:, -128:], routes[...], weights[...], regions)
    depth, _, lanes = out.shape
    high, low = combining(routes[...], weights[...], regions)
    quarter = depth // 4
    rests = [dot(fold_matrix(regions), back[:, (depth + half) * lanes : (depth + half + 1) * lanes]).astype(BF) for half in range(quarter)]
    few = 2 * regions
    for z in range(depth):
        part = z // quarter
        rest = rests[z % quarter][part * few : (part + 1) * few]
        rows = jnp.concatenate([back[:, z * lanes : (z + 1) * lanes], rest], axis=0)
        out[z] = (dot(high, rows, TN) + dot(low, rows, TN)).astype(BF)


def combine_early(back, routes, weights, regions, depth):
    count = routes.shape[1]
    shapes = [jax.ShapeDtypeStruct((depth, count, 2 * EARLY), BF), jax.ShapeDtypeStruct((8, count), F32)]
    return once(functools.partial(combine_early_kernel, regions), shapes, back, routes, weights)


def final_kernel(regions, full, back, own, left, right, tok, gain, squares, sums, routes, weights, moe_out, grad_out, comb_out):
    late = tok.shape[1] - EARLY
    high, low = combining(routes[...], weights[...], regions)
    moe, grad = [dot(high, rows, TN) + dot(low, rows, TN) for rows in decode(back[...], late, fold_matrix(regions))]
    early = own[0].astype(F32) + left[...].astype(F32) + right[...].astype(F32)
    moe_out[:, :late] = moe.astype(BF)
    moe_out[:, late:] = early[:, :EARLY].astype(BF)
    total = sums[...]
    comb_out[...] = total[0:2]
    row = lax.broadcasted_iota(jnp.int32, total.shape, 0)
    columns = jnp.transpose(jnp.where(row == 3, inverse(squares[...], full), total))
    inner, inv = columns[:, 2:3], columns[:, 3:4]
    scaled = gain[...] * jnp.concatenate([grad, early[:, EARLY:]], axis=1)
    grad_out[...] = (inv * scaled - tok[...].astype(F32) * (inv * inv * inv * inner / full)).astype(BF)


def final(back, early, tok, gain, squares, sums, routes, weights, regions, full):
    count, width = tok.shape
    shapes = [
        jax.ShapeDtypeStruct((count, width), BF),
        jax.ShapeDtypeStruct((count, width), BF),
        jax.ShapeDtypeStruct((2, count), F32),
    ]
    kernel = functools.partial(final_kernel, regions, full)
    return once(kernel, shapes, back, *early, tok, gain, squares, sums, routes, weights)


def swap(array, regions):
    split = array.reshape(regions, 8, array.shape[1])
    moved = lax.all_to_all(split, "region", split_axis=0, concat_axis=0, tiled=True)
    return moved.reshape(array.shape)


def add_over_local(array):
    depth = lax.axis_size("local")
    step = 1
    while step < depth:
        array = array + lax.ppermute(array, "local", [(z, z ^ step) for z in range(depth)])
        step *= 2
    return array


def hop(array, step):
    depth = lax.axis_size("local")
    return lax.ppermute(array, "local", [(z, (z + step) % depth) for z in range(depth)])


def ring_gather(own, squares):
    half = lax.axis_size("local") // 2
    low, high = own, own
    blocks = [own]
    for at in range(half - 1):
        low, high = hop(low, 1), hop(high, -1)
        if 1 << at < 2 * half:
            other = lax.ppermute(squares, "local", [(z, z ^ (1 << at)) for z in range(2 * half)])
            low, high, other = lax.optimization_barrier((low, high, other))
            squares = squares + other
        blocks += [low, high]
    at = half - 1
    while 1 << at < 2 * half:
        squares = squares + lax.ppermute(squares, "local", [(z, z ^ (1 << at)) for z in range(2 * half)])
        at += 1
    cut = own.shape[0] // 2
    return blocks + [hop(low[:cut], 1), hop(high[cut:], -1)], squares


def ring_scatter(shares):
    depth = shares.shape[0]
    half = depth // 2
    cut = shares.shape[1] // 2
    right, left = hop(shares[half, :cut], 1), hop(shares[half, cut:], -1)
    add = lambda a, b: (a.astype(F32) + b.astype(F32)).astype(BF)
    right = jnp.concatenate([add(shares[half - 1, :cut], right), shares[half - 1, cut:]], axis=0)
    left = jnp.concatenate([shares[half + 1, :cut], add(shares[half + 1, cut:], left)], axis=0)
    for j in range(half - 2, -1, -1):
        right, left = hop(right, 1), hop(left, -1)
        if j:
            right, left = add(shares[j], right), add(shares[depth - j], left)
    return right, left


def on_device(tokens, norm_gain, w_gate, w_up, w_down, routes, combine, grad_out):
    regions = lax.axis_size("region")
    depth = lax.axis_size("local")
    me = lax.axis_index("local").astype(jnp.int32).reshape(1)
    full = depth * tokens.shape[1]
    gain = norm_gain.reshape(1, -1)
    routes, weights = routes.T, combine.T
    wide = tokens.astype(F32)
    packed, early = pack(tokens, gain, grad_out, routes, regions)
    around, squares = ring_gather(early, jnp.sum(wide * wide, axis=1).reshape(1, -1))
    arrived, _ = lax.optimization_barrier((swap(packed, regions), around[-3]))
    blocks = lax.all_gather(arrived, "local")
    rows = swap(pack_early(around, squares, routes, regions, depth, full), regions)
    hidden = hidden_part(me, blocks, rows, w_gate, w_up, w_down, regions)
    partial, back_rows = back_part(me, *hidden, w_gate, w_up, w_down, regions, depth)
    summed = lax.psum_scatter(partial, "local", scatter_dimension=0)
    shares, sums = combine_early(swap(back_rows, regions), routes, weights, regions, depth)
    own = (shares, *ring_scatter(shares))
    sums = add_over_local(sums)
    moe, grad, comb = final(swap(summed, regions), own, tokens, gain, squares, sums, routes, weights, regions, full)
    return moe, grad, comb.T


def solution(mesh):
    specs = (
        P("region", "local"),
        P("local"),
        P("region", None, "local"),
        P("region", None, "local"),
        P("region", "local", None),
        P("region", None),
        P("region", None),
        P("region", "local"),
    )
    return jax.shard_map(
        on_device,
        mesh=mesh,
        in_specs=specs,
        out_specs=(P("region", "local"), P("region", "local"), P("region", None)),
        check_vma=False,
    )
```

```python
import functools

import jax
import jax.numpy as jnp
from jax import lax
from jax.experimental import pallas as pl
from jax.experimental.pallas import tpu as pltpu
from jax.sharding import PartitionSpec as P

BF = jnp.bfloat16
F32 = jnp.float32
NT = (((1,), (1,)), ((), ()))
TN = (((0,), (0,)), ((), ()))
VMEM_MOST = 63 * 1024 * 1024
VMEM_SOME = 40 * 1024 * 1024
EXTRA = 16
EARLY = 384


def fold_lanes(width):
    return 128 * -(-width // 256)


def packed_lanes(width):
    return 2 * width + fold_lanes(width)


def dot(a, b, dims=(((1,), (0,)), ((), ())), precision=None):
    return lax.dot_general(a, b, dims, precision=precision, preferred_element_type=F32)


def params(limit=VMEM_MOST):
    return pltpu.CompilerParams(vmem_limit_bytes=limit)


def whole(shape):
    return pl.BlockSpec(shape, lambda *_: (0,) * len(shape))


def fold_matrix(regions):
    rows = 8 * regions
    i = lax.broadcasted_iota(jnp.int32, (rows, rows), 0)
    j = lax.broadcasted_iota(jnp.int32, (rows, rows), 1)
    return (j == 4 * (i % (2 * regions)) + i // (2 * regions)).astype(BF)


def encode(main, rest, fold):
    width = main.shape[1] // 2
    lanes = fold_lanes(width)
    pad = 2 * lanes - width
    parts = []
    for side in range(2):
        parts.append(rest[:, side * width : side * width + lanes])
        tail = rest[:, side * width + lanes : (side + 1) * width]
        if pad:
            tail = jnp.concatenate([tail, jnp.zeros((rest.shape[0], pad), rest.dtype)], axis=1)
        parts.append(tail)
    stacked = jnp.concatenate(parts, axis=0)
    return jnp.concatenate([main, dot(fold, stacked, TN).astype(BF)], axis=1)


def decode(block, width, fold):
    lanes = fold_lanes(width)
    rows = block.shape[0]
    rest = dot(fold, block[:, 2 * width :]).astype(BF)
    few = rows // 4
    sides = []
    for side in range(2):
        head = rest[(2 * side) * few : (2 * side + 1) * few]
        tail = rest[(2 * side + 1) * few : (2 * side + 2) * few, : width - lanes]
        low = jnp.concatenate([head, tail], axis=1)
        sides.append(jnp.concatenate([block[:, side * width : (side + 1) * width], low], axis=0))
    return sides


def slot_ids(regions, tokens):
    s = lax.broadcasted_iota(jnp.int32, (10 * regions, tokens), 0)
    late = s - 8 * regions
    expert = jnp.where(late < 0, s // 8, late // 2)
    slot = jnp.where(late < 0, s % 8, 8 + late % 2)
    return expert, slot


def ranks(named):
    count = named.shape[1]
    before = lax.broadcasted_iota(jnp.int32, (count, count), 0)
    after = lax.broadcasted_iota(jnp.int32, (count, count), 1)
    return dot(named.astype(F32).astype(BF), (before < after).astype(F32).astype(BF))


def placed(routes, regions):
    expert, slot = slot_ids(regions, routes.shape[1])
    named = [routes[k : k + 1, :] == expert for k in range(2)]
    at = ranks(named[0] | named[1]) == slot.astype(F32)
    return [n & at for n in named]


def placed_packed(routes, regions):
    s = lax.broadcasted_iota(jnp.int32, (8 * regions, routes.shape[1]), 0)
    expert = s // 8
    named = [routes[k : k + 1, :] == expert for k in range(2)]
    rank = ranks(named[0] | named[1])
    main = rank == (s % 8).astype(F32)
    late = (rank == (8 + (s % 8) // 4).astype(F32)) & (s % 4 == 0)
    return [n & main for n in named], [n & late for n in named]


def once(kernel, out_shape, *operands, limit=VMEM_SOME):
    many = isinstance(out_shape, list)
    specs = [whole(shape.shape) for shape in (out_shape if many else [out_shape])]
    return pl.pallas_call(
        kernel,
        grid=(1,),
        in_specs=[whole(operand.shape) for operand in operands],
        out_specs=specs if many else specs[0],
        out_shape=out_shape,
        compiler_params=params(limit),
    )(*operands)


def triple(value):
    high = value.astype(BF)
    value = value - high.astype(F32)
    middle = value.astype(BF)
    return [high, middle, (value - middle.astype(F32)).astype(BF)]


def in_lanes(columns, rows):
    lane = lax.broadcasted_iota(jnp.int32, (rows, 128), 1)
    out = jnp.zeros((rows, 128), F32)
    for at, column in enumerate(columns):
        if column is not None:
            out = jnp.where(lane == at, column.astype(F32), out)
    return out.astype(BF)


def from_lanes(block, at):
    block = block.astype(F32)
    return block[:, at : at + 1] + block[:, at + 1 : at + 2] + block[:, at + 2 : at + 3]


def in_rows(rows, lanes):
    count = rows[0].shape[1]
    row = lax.broadcasted_iota(jnp.int32, (EXTRA, count), 0)
    out = jnp.zeros((EXTRA, count), F32)
    for at, value in enumerate(rows):
        out = jnp.where(row == at, value.astype(F32), out)
    out = out.astype(BF)
    return jnp.concatenate([out, jnp.zeros((EXTRA, lanes - count), BF)], axis=1)


def pack_kernel(regions, tok, gain, grad, routes, out, early):
    at = placed(routes[...], regions)
    pick = (at[0] | at[1]).astype(F32).astype(BF)
    late = out.shape[1] * 2 // 5
    count = tok.shape[0]
    wide = tok[...].astype(F32)
    scaled = (wide * gain[...]).astype(BF)
    rows = dot(pick, jnp.concatenate([scaled[:, :late], grad[:, :late]], axis=1)).astype(BF)
    cut = 8 * regions
    out[...] = encode(rows[:cut], rows[cut:], fold_matrix(regions))
    early[:count] = jnp.concatenate([scaled[:, late:], grad[:, late:]], axis=1)
    squares = jnp.broadcast_to(jnp.sum(wide * wide, axis=1, keepdims=True), (count, 128))
    early[count:] = in_rows(triple(jnp.transpose(squares)[0:1]), early.shape[1])


def pack(tok, gain, grad, routes, regions):
    count, width = tok.shape
    shapes = [
        jax.ShapeDtypeStruct((8 * regions, packed_lanes(width - EARLY)), BF),
        jax.ShapeDtypeStruct((count + EXTRA, 2 * EARLY), BF),
    ]
    return once(functools.partial(pack_kernel, regions), shapes, tok, gain, grad, routes, limit=VMEM_MOST)


def inverse(squares, full):
    return lax.rsqrt(squares / full + 1e-06)


def pack_early_kernel(regions, depth, full, routes, *refs):
    blocks, out = refs[:-1], refs[-1]
    lanes = blocks[0].shape[1]
    early = {0: blocks[0][...]}
    half = depth // 2
    for hop in range(1, half):
        early[depth - hop] = blocks[2 * hop - 1][...]
        early[hop] = blocks[2 * hop][...]
    early[half] = jnp.concatenate([blocks[-2][...], blocks[-1][...]], axis=0)
    at = placed(routes[...], regions)
    pick = (at[0] | at[1]).astype(F32).astype(BF)
    cut = 8 * regions
    rests = []
    count = routes.shape[1]
    squares = 0.0
    for z in range(depth):
        rows = dot(pick, early[z][:count]).astype(BF)
        extra = early[z][count:, :count].astype(F32)
        squares = squares + extra[0:1] + extra[1:2] + extra[2:3]
        out[:, z * lanes : (z + 1) * lanes] = rows[:cut]
        rests.append(rows[cut:])
    for half in range(depth // 4):
        stacked = jnp.concatenate([rests[part * (depth // 4) + half] for part in range(4)], axis=0)
        at_lane = (depth + half) * lanes
        out[:, at_lane : at_lane + lanes] = dot(fold_matrix(regions), stacked, TN).astype(BF)
    inv = inverse(squares, full)
    columns = []
    for found in placed_packed(routes[...], regions):
        columns += triple(jnp.sum(jnp.where(found[0] | found[1], inv, 0.0), axis=1, keepdims=True))
    out[:, -128:] = in_lanes(columns, cut)


def early_shape(regions, depth):
    return (8 * regions, 2 * EARLY * depth * 5 // 4 + 128)


def pack_early(blocks, routes, regions, depth, full):
    shape = jax.ShapeDtypeStruct(early_shape(regions, depth), BF)
    return once(functools.partial(pack_early_kernel, regions, depth, full), shape, routes, *blocks)


def relative_specs(width, units, depth):
    return [
        pl.BlockSpec((1, width, units), lambda z, me: (0, (z + me[0]) % depth, 0)),
        pl.BlockSpec((1, width, units), lambda z, me: (0, (z + me[0]) % depth, 0)),
        pl.BlockSpec((1, units, width), lambda z, me: (0, 0, (z + me[0]) % depth)),
    ]


def hidden_kernel(
    regions, me, scales, block, main, rest, gate_w, up_w, down_w, hid_out, gate_out, up_out, scal_out, acc_g, acc_u, acc_h, fold
):
    step = pl.program_id(0)
    width = gate_w.shape[1]
    few = 2 * regions
    quarter = pl.num_programs(0) // 4

    @pl.when(step == 0)
    def _():
        fold[...] = fold_matrix(regions)
        acc_g[...] = jnp.zeros_like(acc_g)
        acc_u[...] = jnp.zeros_like(acc_u)
        acc_h[...] = jnp.zeros_like(acc_h)

    late_in, late_grad = decode(block[0], width - EARLY, fold[...])
    pick = fold[pl.ds(pl.multiple_of((step // quarter) * few, few), few), :]
    early = jnp.concatenate([main[...], dot(pick, rest[...]).astype(BF)], axis=0)
    rows_in = jnp.concatenate([late_in, early[:, :EARLY]], axis=1)
    rows_grad = jnp.concatenate([late_grad, early[:, EARLY:]], axis=1)
    acc_g[...] += dot(rows_in, gate_w[0])
    acc_u[...] += dot(rows_in, up_w[0])
    acc_h[...] += dot(rows_grad, down_w[0], NT)

    @pl.when(step == pl.num_programs(0) - 1)
    def _():
        cut = 8 * regions
        first = fold[0:few, :]
        inv = jnp.concatenate([from_lanes(scales[...], 0), from_lanes(dot(first, scales[...]), 3)], axis=0)
        gate_raw, up_raw, grad_hidden = acc_g[...], acc_u[...], acc_h[...]
        gate_pre, up_pre = gate_raw * inv, up_raw * inv
        sig = jax.nn.sigmoid(gate_pre)
        act = gate_pre * sig
        hidden = (act * up_pre).astype(BF)
        grad_gate = (grad_hidden * up_pre * sig * (1.0 + gate_pre * (1.0 - sig))).astype(BF)
        grad_up = (grad_hidden * act).astype(BF)
        hid_out[...] = hidden
        gate_out[...] = grad_gate
        up_out[...] = grad_up
        comb = jnp.sum(hidden.astype(F32) * grad_hidden, axis=1, keepdims=True)
        inner = jnp.sum(grad_gate.astype(F32) * gate_raw + grad_up.astype(F32) * up_raw, axis=1, keepdims=True)
        here = in_lanes(triple(comb[:cut]) + triple(inner[:cut]), cut)
        there = in_lanes([None] * 6 + triple(comb[cut:]) + triple(inner[cut:]), few)
        scal_out[...] = here + dot(first, there, TN).astype(BF)


def hidden_part(me, blocks, rows, gate_w, up_w, down_w, regions):
    depth, cut, lanes = blocks.shape
    width, units = gate_w.shape[1] // depth, gate_w.shape[2]
    total = 10 * regions
    return pl.pallas_call(
        functools.partial(hidden_kernel, regions),
        grid_spec=pltpu.PrefetchScalarGridSpec(
            num_scalar_prefetch=1,
            grid=(depth,),
            in_specs=[
                pl.BlockSpec((cut, 128), lambda z, me: (0, 2 * EARLY * depth * 5 // 512)),
                pl.BlockSpec((1, cut, lanes), lambda z, me: ((z + me[0]) % depth, 0, 0)),
                pl.BlockSpec((cut, 2 * EARLY), lambda z, me: (0, z)),
                pl.BlockSpec((cut, 2 * EARLY), lambda z, me: (0, depth + z % (depth // 4))),
            ]
            + relative_specs(width, units, depth),
            out_specs=[whole((total, units))] * 3 + [whole((cut, 128))],
            scratch_shapes=[pltpu.VMEM((total, units), F32)] * 3 + [pltpu.VMEM((cut, cut), BF)],
        ),
        out_shape=[jax.ShapeDtypeStruct((total, units), BF)] * 3 + [jax.ShapeDtypeStruct((cut, 128), BF)],
        compiler_params=params(),
    )(me, rows, blocks, rows, rows, gate_w, up_w, down_w)


def back_kernel(regions, me, hid, gate_g, up_g, scal, gate_w, up_w, down_w, late_out, early_out, fold):
    depth = pl.num_programs(0)
    step = pl.program_id(0)
    late = gate_w.shape[1] - EARLY
    lanes = 2 * EARLY
    few = 2 * regions
    cut = 8 * regions
    quarter = depth // 4

    @pl.when(step == 0)
    def _():
        fold[...] = fold_matrix(regions)
        early_out[:, -128:] = scal[...]

    moe = dot(hid[...], down_w[0]).astype(BF)
    grad = (dot(gate_g[...], gate_w[0], NT) + dot(up_g[...], up_w[0], NT)).astype(BF)
    both = jnp.concatenate([moe[:, :late], grad[:, :late]], axis=1)
    late_out[0] = encode(both[:cut], both[cut:], fold[...])
    both = jnp.concatenate([moe[:, late:], grad[:, late:]], axis=1)
    early_out[:, pl.ds(pl.multiple_of(step * lanes, 128), lanes)] = both[:cut]
    spot = pl.ds(pl.multiple_of((depth + step % quarter) * lanes, 128), lanes)
    pick = fold[pl.ds(pl.multiple_of((step // quarter) * few, few), few), :]
    low = dot(pick, both[cut:], TN).astype(BF)

    @pl.when(step < quarter)
    def _():
        early_out[:, spot] = low

    @pl.when(step >= quarter)
    def _():
        early_out[:, spot] = early_out[:, spot] + low


def back_part(me, hid, gate_g, up_g, scal, gate_w, up_w, down_w, regions, depth):
    width, units = gate_w.shape[1] // depth, gate_w.shape[2]
    total = 10 * regions
    cut = 8 * regions
    lanes = packed_lanes(width - EARLY)
    shape = early_shape(regions, depth)
    return pl.pallas_call(
        functools.partial(back_kernel, regions),
        grid_spec=pltpu.PrefetchScalarGridSpec(
            num_scalar_prefetch=1,
            grid=(depth,),
            in_specs=[whole((total, units))] * 3 + [whole((cut, 128))] + relative_specs(width, units, depth),
            out_specs=[pl.BlockSpec((1, cut, lanes), lambda z, me: ((z + me[0]) % depth, 0, 0)), whole(shape)],
            scratch_shapes=[pltpu.VMEM((cut, cut), BF)],
        ),
        out_shape=[jax.ShapeDtypeStruct((depth, cut, lanes), BF), jax.ShapeDtypeStruct(shape, BF)],
        compiler_params=params(),
    )(me, hid, gate_g, up_g, scal, gate_w, up_w, down_w)


def scalars(here, routes, weights, regions):
    main, late = placed_packed(routes, regions)
    parts = []
    inner = 0.0
    for k in range(2):
        comb = jnp.where(main[k], from_lanes(here, 0), 0.0) + jnp.where(late[k], from_lanes(here, 6), 0.0)
        part = jnp.where(main[k], from_lanes(here, 3), 0.0) + jnp.where(late[k], from_lanes(here, 9), 0.0)
        parts.append(jnp.sum(comb, axis=0, keepdims=True))
        inner = inner + weights[k : k + 1, :] * jnp.sum(part, axis=0, keepdims=True)
    return parts + [inner]


def combining(routes, weights, regions):
    at = placed(routes, regions)
    weight = jnp.where(at[0], weights[0:1, :], 0.0) + jnp.where(at[1], weights[1:2, :], 0.0)
    high = weight.astype(BF)
    return high, (weight - high.astype(F32)).astype(BF)


def combine_early_kernel(regions, squares, back, routes, weights, out, right, left):
    depth, rows_out, lanes = out.shape
    count = rows_out - EXTRA
    high, low = combining(routes[...], weights[...], regions)
    quarter = depth // 4
    few = 2 * regions
    values = []
    for value in scalars(back[:, -128:], routes[...], weights[...], regions):
        values += triple(value)
    count = routes.shape[1]
    values += [squares[at : at + 1, :count] for at in range(3)]
    extra = in_rows(values, lanes)
    fold = fold_matrix(regions)
    rests = [dot(fold, back[:, (depth + half) * lanes : (depth + half + 1) * lanes]).astype(BF) for half in range(quarter)]
    for z in range(depth):
        part = z // quarter
        rest = rests[z % quarter][part * few : (part + 1) * few]
        rows = jnp.concatenate([back[:, z * lanes : (z + 1) * lanes], rest], axis=0)
        share = (dot(high, rows, TN) + dot(low, rows, TN)).astype(BF)
        out[z, :count] = share
        out[z, count:] = extra
        if z == depth // 2:
            right[...] = jnp.concatenate([share[: count // 2], extra], axis=0)
            left[...] = jnp.concatenate([share[count // 2 :], extra], axis=0)


def combine_early(early, back, routes, weights, regions, depth):
    count = routes.shape[1]
    squares = early[count:]
    lanes = 2 * EARLY
    shapes = [
        jax.ShapeDtypeStruct((depth, count + EXTRA, lanes), BF),
        jax.ShapeDtypeStruct((count // 2 + EXTRA, lanes), BF),
        jax.ShapeDtypeStruct((count // 2 + EXTRA, lanes), BF),
    ]
    return once(functools.partial(combine_early_kernel, regions), shapes, squares, back, routes, weights)


def forward_kernel(for_right, for_left, right, left, right_out, left_out):
    rows = for_right.shape[1]
    count = rows - EXTRA
    arrived = right.shape[0] - EXTRA
    for own, got, out, start in ((for_right, right, right_out, 0), (for_left, left, left_out, count - arrived)):
        if arrived < count:
            out[:count] = own[0, :count]
        spot = slice(start, start + arrived)
        out[spot] = (own[0, spot].astype(F32) + got[:arrived].astype(F32)).astype(BF)
        out[count:] = jnp.concatenate([own[0, count:, :128], got[arrived:, :-128]], axis=1)


def forward(shares, at, right, left):
    depth, rows, lanes = shares.shape
    shape = jax.ShapeDtypeStruct((rows, lanes), BF)
    return pl.pallas_call(
        forward_kernel,
        grid=(1,),
        in_specs=[
            pl.BlockSpec((1, rows, lanes), lambda _: (at, 0, 0)),
            pl.BlockSpec((1, rows, lanes), lambda _: (depth - at, 0, 0)),
            whole(right.shape),
            whole(left.shape),
        ],
        out_specs=[whole((rows, lanes))] * 2,
        out_shape=[shape, shape],
        compiler_params=params(VMEM_SOME),
    )(shares, shares, right, left)


def final_kernel(regions, full, depth, me, back, own, right, left, tok, gain, routes, weights, moe_out, grad_out, comb_out, stack):
    count = tok.shape[0]
    late = tok.shape[1] - EARLY
    high, low = combining(routes[...], weights[...], regions)
    moe, grad = [dot(high, rows, TN) + dot(low, rows, TN) for rows in decode(back[...], late, fold_matrix(regions))]
    early = own[0, :count].astype(F32) + right[:count].astype(F32) + left[:count].astype(F32)
    moe_out[:, :late] = moe.astype(BF)
    moe_out[:, late:] = early[:, :EARLY].astype(BF)
    wide = tok[...].astype(F32)
    stack[0] = own[0, count:, :count].astype(F32)
    for away in range(1, depth):
        source, slot = (left, away - 1) if away <= depth // 2 else (right, depth - away - 1)
        stack[away] = source[count:, slot * 128 : slot * 128 + count].astype(F32)
    total = 0.0
    for z in range(depth):
        total = total + stack[(z - me[0] + depth) % depth]
    comb = [total[3 * k : 3 * k + 1] + total[3 * k + 1 : 3 * k + 2] + total[3 * k + 2 : 3 * k + 3] for k in range(3)]
    comb_out[0:1] = comb[0]
    comb_out[1:2] = comb[1]
    inv = inverse(total[9:10] + total[10:11] + total[11:12], full)
    row = lax.broadcasted_iota(jnp.int32, (8, count), 0)
    columns = jnp.transpose(jnp.where(row == 0, comb[2], jnp.where(row == 1, inv, 0.0)))
    inner, inv = columns[:, 0:1], columns[:, 1:2]
    scaled = gain[...] * jnp.concatenate([grad, early[:, EARLY:]], axis=1)
    grad_out[...] = (inv * scaled - wide * (inv * inv * inv * inner / full)).astype(BF)


def final(me, back, shares, right, left, tok, gain, routes, weights, regions, full):
    count, width = tok.shape
    depth, rows, lanes = shares.shape
    shapes = [
        jax.ShapeDtypeStruct((count, width), BF),
        jax.ShapeDtypeStruct((count, width), BF),
        jax.ShapeDtypeStruct((2, count), F32),
    ]
    operands = (back, shares, right, left, tok, gain, routes, weights)
    specs = [whole(operand.shape) for operand in operands]
    specs[1] = pl.BlockSpec((1, rows, lanes), lambda *_: (0, 0, 0))
    return pl.pallas_call(
        functools.partial(final_kernel, regions, full, depth),
        grid_spec=pltpu.PrefetchScalarGridSpec(
            num_scalar_prefetch=1,
            grid=(1,),
            in_specs=specs,
            out_specs=[whole(shape.shape) for shape in shapes],
            scratch_shapes=[pltpu.VMEM((depth, EXTRA, count), F32)],
        ),
        out_shape=shapes,
        compiler_params=params(VMEM_SOME),
    )(me, *operands)


def swap(array, regions):
    split = array.reshape(regions, 8, array.shape[1])
    moved = lax.all_to_all(split, "region", split_axis=0, concat_axis=0, tiled=True)
    return moved.reshape(array.shape)


def hop(array, step):
    depth = lax.axis_size("local")
    return lax.ppermute(array, "local", [(z, (z + step) % depth) for z in range(depth)])


def ring_gather(own, packed):
    half = lax.axis_size("local") // 2
    low, high = own, own
    blocks = [own]
    for at in range(half - 1):
        low, high = lax.optimization_barrier((hop(low, 1), hop(high, -1)))
        if at == 0:
            low, high, packed = lax.optimization_barrier((low, high, packed))
        blocks += [low, high]
    cut = (own.shape[0] - EXTRA) // 2
    return blocks + [hop(low[:cut], 1), hop(high[cut:], -1)], packed


def ring_scatter(shares, right, left):
    for at in range(shares.shape[0] // 2 - 1, -1, -1):
        right, left = hop(right, 1), hop(left, -1)
        if at:
            right, left = forward(shares, at, right, left)
    return right, left


def on_device(tokens, norm_gain, w_gate, w_up, w_down, routes, combine, grad_out):
    regions = lax.axis_size("region")
    depth = lax.axis_size("local")
    me = lax.axis_index("local").astype(jnp.int32).reshape(1)
    full = depth * tokens.shape[1]
    gain = norm_gain.reshape(1, -1)
    routes, weights = routes.T, combine.T
    packed, early = pack(tokens, gain, grad_out, routes, regions)
    around, packed = ring_gather(early, packed)
    arrived, _ = lax.optimization_barrier((swap(packed, regions), around[-3]))
    blocks = lax.all_gather(arrived, "local")
    rows = swap(pack_early(around, routes, regions, depth, full), regions)
    hidden = hidden_part(me, blocks, rows, w_gate, w_up, w_down, regions)
    partial, back_rows = back_part(me, *hidden, w_gate, w_up, w_down, regions, depth)
    summed = lax.psum_scatter(partial, "local", scatter_dimension=0)
    shares, right, left = combine_early(early, swap(back_rows, regions), routes, weights, regions, depth)
    right, left = ring_scatter(shares, right, left)
    moe, grad, comb = final(me, swap(summed, regions), shares, right, left, tokens, gain, routes, weights, regions, full)
    return moe, grad, comb.T


def solution(mesh):
    specs = (
        P("region", "local"),
        P("local"),
        P("region", None, "local"),
        P("region", None, "local"),
        P("region", "local", None),
        P("region", None),
        P("region", None),
        P("region", "local"),
    )
    return jax.shard_map(
        on_device,
        mesh=mesh,
        in_specs=specs,
        out_specs=(P("region", "local"), P("region", "local"), P("region", None)),
        check_vma=False,
    )
```

```python
import functools

import jax
import jax.numpy as jnp
from jax import lax
from jax.experimental import pallas as pl
from jax.experimental.pallas import tpu as pltpu
from jax.sharding import PartitionSpec as P

BF = jnp.bfloat16
F32 = jnp.float32
NT = (((1,), (1,)), ((), ()))
TN = (((0,), (0,)), ((), ()))
VMEM_MOST = 63 * 1024 * 1024
VMEM_SOME = 40 * 1024 * 1024
EXTRA = 16
EARLY = 384


def fold_lanes(width):
    return 128 * -(-width // 256)


def packed_lanes(width):
    return 2 * width + fold_lanes(width)


def dot(a, b, dims=(((1,), (0,)), ((), ())), precision=None):
    return lax.dot_general(a, b, dims, precision=precision, preferred_element_type=F32)


def params(limit=VMEM_MOST):
    return pltpu.CompilerParams(vmem_limit_bytes=limit)


def whole(shape):
    return pl.BlockSpec(shape, lambda *_: (0,) * len(shape))


def fold_matrix(regions):
    rows = 8 * regions
    i = lax.broadcasted_iota(jnp.int32, (rows, rows), 0)
    j = lax.broadcasted_iota(jnp.int32, (rows, rows), 1)
    return (j == 4 * (i % (2 * regions)) + i // (2 * regions)).astype(BF)


def encode(main, rest, fold):
    width = main.shape[1] // 2
    lanes = fold_lanes(width)
    pad = 2 * lanes - width
    parts = []
    for side in range(2):
        parts.append(rest[:, side * width : side * width + lanes])
        tail = rest[:, side * width + lanes : (side + 1) * width]
        if pad:
            tail = jnp.concatenate([tail, jnp.zeros((rest.shape[0], pad), rest.dtype)], axis=1)
        parts.append(tail)
    stacked = jnp.concatenate(parts, axis=0)
    return jnp.concatenate([main, dot(fold, stacked, TN).astype(BF)], axis=1)


def decode(block, width, fold):
    lanes = fold_lanes(width)
    rows = block.shape[0]
    rest = dot(fold, block[:, 2 * width :]).astype(BF)
    few = rows // 4
    sides = []
    for side in range(2):
        head = rest[(2 * side) * few : (2 * side + 1) * few]
        tail = rest[(2 * side + 1) * few : (2 * side + 2) * few, : width - lanes]
        low = jnp.concatenate([head, tail], axis=1)
        sides.append(jnp.concatenate([block[:, side * width : (side + 1) * width], low], axis=0))
    return sides


def slot_ids(regions, tokens):
    s = lax.broadcasted_iota(jnp.int32, (10 * regions, tokens), 0)
    late = s - 8 * regions
    expert = jnp.where(late < 0, s // 8, late // 2)
    slot = jnp.where(late < 0, s % 8, 8 + late % 2)
    return expert, slot


def ranks(named):
    count = named.shape[1]
    before = lax.broadcasted_iota(jnp.int32, (count, count), 0)
    after = lax.broadcasted_iota(jnp.int32, (count, count), 1)
    return dot(named.astype(F32).astype(BF), (before < after).astype(F32).astype(BF))


def placed(routes, regions):
    expert, slot = slot_ids(regions, routes.shape[1])
    named = [routes[k : k + 1, :] == expert for k in range(2)]
    at = ranks(named[0] | named[1]) == slot.astype(F32)
    return [n & at for n in named]


def placed_packed(routes, regions):
    s = lax.broadcasted_iota(jnp.int32, (8 * regions, routes.shape[1]), 0)
    expert = s // 8
    named = [routes[k : k + 1, :] == expert for k in range(2)]
    rank = ranks(named[0] | named[1])
    main = rank == (s % 8).astype(F32)
    late = (rank == (8 + (s % 8) // 4).astype(F32)) & (s % 4 == 0)
    return [n & main for n in named], [n & late for n in named]


def once(kernel, out_shape, *operands, limit=VMEM_SOME):
    many = isinstance(out_shape, list)
    specs = [whole(shape.shape) for shape in (out_shape if many else [out_shape])]
    return pl.pallas_call(
        kernel,
        grid=(1,),
        in_specs=[whole(operand.shape) for operand in operands],
        out_specs=specs if many else specs[0],
        out_shape=out_shape,
        compiler_params=params(limit),
    )(*operands)


def triple(value):
    high = value.astype(BF)
    value = value - high.astype(F32)
    middle = value.astype(BF)
    return [high, middle, (value - middle.astype(F32)).astype(BF)]


def in_lanes(columns, rows):
    lane = lax.broadcasted_iota(jnp.int32, (rows, 128), 1)
    out = jnp.zeros((rows, 128), F32)
    for at, column in enumerate(columns):
        if column is not None:
            out = jnp.where(lane == at, column.astype(F32), out)
    return out.astype(BF)


def from_lanes(block, at):
    block = block.astype(F32)
    return block[:, at : at + 1] + block[:, at + 1 : at + 2] + block[:, at + 2 : at + 3]


def in_rows(rows, lanes):
    count = rows[0].shape[1]
    row = lax.broadcasted_iota(jnp.int32, (EXTRA, count), 0)
    out = jnp.zeros((EXTRA, count), F32)
    for at, value in enumerate(rows):
        out = jnp.where(row == at, value.astype(F32), out)
    out = out.astype(BF)
    return jnp.concatenate([out, jnp.zeros((EXTRA, lanes - count), BF)], axis=1)


def pack_kernel(regions, tok, gain, grad, routes, out, early):
    at = placed(routes[...], regions)
    pick = (at[0] | at[1]).astype(F32).astype(BF)
    late = out.shape[1] * 2 // 5
    count = tok.shape[0]
    wide = tok[...].astype(F32)
    scaled = (wide * gain[...].reshape(1, -1)).astype(BF)
    rows = dot(pick, jnp.concatenate([scaled[:, :late], grad[:, :late]], axis=1)).astype(BF)
    cut = 8 * regions
    out[...] = encode(rows[:cut], rows[cut:], fold_matrix(regions))
    early[:count] = jnp.concatenate([scaled[:, late:], grad[:, late:]], axis=1)
    squares = jnp.broadcast_to(jnp.sum(wide * wide, axis=1, keepdims=True), (count, 128))
    early[count:] = in_rows(triple(jnp.transpose(squares)[0:1]), early.shape[1])


def pack(tok, gain, grad, routes, regions):
    count, width = tok.shape
    shapes = [
        jax.ShapeDtypeStruct((8 * regions, packed_lanes(width - EARLY)), BF),
        jax.ShapeDtypeStruct((count + EXTRA, 2 * EARLY), BF),
    ]
    return once(functools.partial(pack_kernel, regions), shapes, tok, gain, grad, routes, limit=VMEM_MOST)


def inverse(squares, full):
    return lax.rsqrt(squares / full + 1e-06)


def pack_early_kernel(regions, depth, full, routes, *refs):
    blocks, out = refs[:-1], refs[-1]
    lanes = blocks[0].shape[1]
    early = {0: blocks[0][...]}
    half = depth // 2
    for hop in range(1, half):
        early[depth - hop] = blocks[2 * hop - 1][...]
        early[hop] = blocks[2 * hop][...]
    early[half] = jnp.concatenate([blocks[-2][...], blocks[-1][...]], axis=0)
    at = placed(routes[...], regions)
    pick = (at[0] | at[1]).astype(F32).astype(BF)
    cut = 8 * regions
    rests = []
    count = routes.shape[1]
    squares = 0.0
    for z in range(depth):
        rows = dot(pick, early[z][:count]).astype(BF)
        extra = early[z][count:, :count].astype(F32)
        squares = squares + extra[0:1] + extra[1:2] + extra[2:3]
        out[:, z * lanes : (z + 1) * lanes] = rows[:cut]
        rests.append(rows[cut:])
    for half in range(depth // 4):
        stacked = jnp.concatenate(rests[4 * half : 4 * half + 4], axis=0)
        at_lane = (depth + half) * lanes
        out[:, at_lane : at_lane + lanes] = dot(fold_matrix(regions), stacked, TN).astype(BF)
    inv = inverse(squares, full)
    columns = []
    for found in placed_packed(routes[...], regions):
        columns += triple(jnp.sum(jnp.where(found[0] | found[1], inv, 0.0), axis=1, keepdims=True))
    out[:, -128:] = in_lanes(columns, cut)


def early_shape(regions, depth):
    return (8 * regions, 2 * EARLY * depth * 5 // 4 + 128)


def pack_early(blocks, routes, regions, depth, full):
    shape = jax.ShapeDtypeStruct(early_shape(regions, depth), BF)
    return once(functools.partial(pack_early_kernel, regions, depth, full), shape, routes, *blocks)


def anywhere():
    return pl.BlockSpec(memory_space=pl.ANY)


def expert_kernel(
    regions,
    depth,
    me,
    blocks,
    rows,
    gate_hbm,
    up_hbm,
    down_hbm,
    late_out,
    early_out,
    gate_w,
    up_w,
    down_w,
    acc_g,
    acc_u,
    acc_h,
    hid,
    gate_g,
    up_g,
    scal,
    fold,
    scales,
    sem,
    weight_sems,
):
    width = gate_w.shape[1] // depth
    few = 2 * regions
    cut, lanes = blocks.shape[1:]
    first_block = me[0]
    copy = pltpu.make_async_copy(rows.at[:, rows.shape[1] - 128 :], scales, sem)
    copy.start()

    def lanes_of(step):
        return pl.ds(pl.multiple_of((step + first_block) % depth * width, 128), width)

    def weight_copies(step):
        at = lanes_of(step)
        return [
            pltpu.make_async_copy(gate_hbm.at[:, at, :], gate_w.at[:, at, :], weight_sems.at[0, step]),
            pltpu.make_async_copy(up_hbm.at[:, at, :], up_w.at[:, at, :], weight_sems.at[1, step]),
            pltpu.make_async_copy(down_hbm.at[:, :, at], down_w.at[:, :, at], weight_sems.at[2, step]),
        ]

    for step in range(depth):
        for one in weight_copies(step):
            one.start()
    fold[...] = fold_matrix(regions)
    acc_g[...] = jnp.zeros_like(acc_g)
    acc_u[...] = jnp.zeros_like(acc_u)
    acc_h[...] = jnp.zeros_like(acc_h)

    def body(block, main, rest):
        step = pl.program_id(0)
        at = lanes_of(step)
        for one in weight_copies(step):
            one.wait()
        late_in, late_grad = decode(block[0], width - EARLY, fold[...])
        pick = fold[pl.ds(pl.multiple_of((step % 4) * few, few), few), :]
        early = jnp.concatenate([main[...], dot(pick, rest[...]).astype(BF)], axis=0)
        rows_in = jnp.concatenate([late_in, early[:, :EARLY]], axis=1)
        rows_grad = jnp.concatenate([late_grad, early[:, EARLY:]], axis=1)
        acc_g[...] += dot(rows_in, gate_w[0, at, :])
        acc_u[...] += dot(rows_in, up_w[0, at, :])
        acc_h[...] += dot(rows_grad, down_w[0, :, at], NT)

    pltpu.emit_pipeline(
        body,
        grid=(depth,),
        in_specs=[
            pl.BlockSpec((1, cut, lanes), lambda z: ((z + first_block) % depth, 0, 0)),
            pl.BlockSpec((cut, 2 * EARLY), lambda z: (0, z)),
            pl.BlockSpec((cut, 2 * EARLY), lambda z: (0, depth + z // 4)),
        ],
    )(blocks, rows, rows)

    copy.wait()
    first = fold[0:few, :]
    inv = jnp.concatenate([from_lanes(scales[...], 0), from_lanes(dot(first, scales[...]), 3)], axis=0)
    gate_raw, up_raw, grad_hidden = acc_g[...], acc_u[...], acc_h[...]
    gate_pre, up_pre = gate_raw * inv, up_raw * inv
    sig = jax.nn.sigmoid(gate_pre)
    act = gate_pre * sig
    hidden = (act * up_pre).astype(BF)
    grad_gate = (grad_hidden * up_pre * sig * (1.0 + gate_pre * (1.0 - sig))).astype(BF)
    grad_up = (grad_hidden * act).astype(BF)
    hid[...] = hidden
    gate_g[...] = grad_gate
    up_g[...] = grad_up
    comb = jnp.sum(hidden.astype(F32) * grad_hidden, axis=1, keepdims=True)
    inner = jnp.sum(grad_gate.astype(F32) * gate_raw + grad_up.astype(F32) * up_raw, axis=1, keepdims=True)
    here = in_lanes(triple(comb[:cut]) + triple(inner[:cut]), cut)
    there = in_lanes([None] * 6 + triple(comb[cut:]) + triple(inner[cut:]), few)
    scal[...] = here + dot(first, there, TN).astype(BF)
    late = width - EARLY
    late_lanes = late_out.shape[2]

    def back(late_block, main, rest):
        step = pl.program_id(0)
        at = lanes_of(step)
        moe = dot(hid[...], down_w[0, :, at]).astype(BF)
        grad = (dot(gate_g[...], gate_w[0, at, :], NT) + dot(up_g[...], up_w[0, at, :], NT)).astype(BF)
        both = jnp.concatenate([moe[:, :late], grad[:, :late]], axis=1)
        late_block[0] = encode(both[:cut], both[cut:], fold[...])
        both = jnp.concatenate([moe[:, late:], grad[:, late:]], axis=1)
        main[...] = both[:cut]
        pick = fold[pl.ds(pl.multiple_of((step % 4) * few, few), few), :]
        low = dot(pick, both[cut:], TN).astype(BF)

        @pl.when(step % 4 == 0)
        def _():
            rest[...] = low

        @pl.when(step % 4 > 0)
        def _():
            rest[...] = rest[...] + low

    pltpu.emit_pipeline(
        back,
        grid=(depth,),
        out_specs=[
            pl.BlockSpec((1, cut, late_lanes), lambda z: ((z + first_block) % depth, 0, 0)),
            pl.BlockSpec((cut, 2 * EARLY), lambda z: (0, z)),
            pl.BlockSpec((cut, 2 * EARLY), lambda z: (0, depth + z // 4)),
        ],
    )(late_out, early_out, early_out)
    pltpu.sync_copy(scal, early_out.at[:, early_out.shape[1] - 128 :])


def expert_part(me, blocks, rows, gate_w, up_w, down_w, regions):
    depth, cut, lanes = blocks.shape
    units = gate_w.shape[2]
    total = 10 * regions
    return pl.pallas_call(
        functools.partial(expert_kernel, regions, depth),
        in_specs=[pl.BlockSpec(memory_space=pltpu.SMEM)] + [anywhere()] * 5,
        out_specs=[anywhere()] * 2,
        out_shape=[jax.ShapeDtypeStruct((depth, cut, lanes), BF), jax.ShapeDtypeStruct(rows.shape, BF)],
        scratch_shapes=[pltpu.VMEM(w.shape, BF) for w in (gate_w, up_w, down_w)]
        + [pltpu.VMEM((total, units), F32)] * 3
        + [pltpu.VMEM((total, units), BF)] * 3
        + [pltpu.VMEM((cut, 128), BF), pltpu.VMEM((cut, cut), BF), pltpu.VMEM((cut, 128), BF)]
        + [pltpu.SemaphoreType.DMA(()), pltpu.SemaphoreType.DMA((3, depth))],
        compiler_params=params(VMEM_MOST),
    )(me, blocks, rows, gate_w, up_w, down_w)


def scalars(here, routes, weights, regions):
    main, late = placed_packed(routes, regions)
    parts = []
    inner = 0.0
    for k in range(2):
        comb = jnp.where(main[k], from_lanes(here, 0), 0.0) + jnp.where(late[k], from_lanes(here, 6), 0.0)
        part = jnp.where(main[k], from_lanes(here, 3), 0.0) + jnp.where(late[k], from_lanes(here, 9), 0.0)
        parts.append(jnp.sum(comb, axis=0, keepdims=True))
        inner = inner + weights[k : k + 1, :] * jnp.sum(part, axis=0, keepdims=True)
    return parts + [inner]


def combining(routes, weights, regions):
    at = placed(routes, regions)
    weight = jnp.where(at[0], weights[0:1, :], 0.0) + jnp.where(at[1], weights[1:2, :], 0.0)
    high = weight.astype(BF)
    return high, (weight - high.astype(F32)).astype(BF)


def combine_early_kernel(regions, squares, back, routes, weights, out, right, left):
    depth, rows_out, lanes = out.shape
    count = rows_out - EXTRA
    high, low = combining(routes[...], weights[...], regions)
    quarter = depth // 4
    few = 2 * regions
    values = []
    for value in scalars(back[:, -128:], routes[...], weights[...], regions):
        values += triple(value)
    count = routes.shape[1]
    values += [squares[at : at + 1, :count] for at in range(3)]
    extra = in_rows(values, lanes)
    fold = fold_matrix(regions)
    rests = [dot(fold, back[:, (depth + half) * lanes : (depth + half + 1) * lanes]).astype(BF) for half in range(quarter)]
    for z in range(depth):
        part = z % 4
        rest = rests[z // 4][part * few : (part + 1) * few]
        rows = jnp.concatenate([back[:, z * lanes : (z + 1) * lanes], rest], axis=0)
        share = (dot(high, rows, TN) + dot(low, rows, TN)).astype(BF)
        out[z, :count] = share
        out[z, count:] = extra
        if z == depth // 2:
            right[...] = jnp.concatenate([share[: count // 2], extra], axis=0)
            left[...] = jnp.concatenate([share[count // 2 :], extra], axis=0)


def combine_early(early, back, routes, weights, regions, depth):
    count = routes.shape[1]
    squares = early[count:]
    lanes = 2 * EARLY
    shapes = [
        jax.ShapeDtypeStruct((depth, count + EXTRA, lanes), BF),
        jax.ShapeDtypeStruct((count // 2 + EXTRA, lanes), BF),
        jax.ShapeDtypeStruct((count // 2 + EXTRA, lanes), BF),
    ]
    return once(functools.partial(combine_early_kernel, regions), shapes, squares, back, routes, weights)


def forward_kernel(for_right, for_left, right, left, right_out, left_out):
    rows = for_right.shape[1]
    count = rows - EXTRA
    arrived = right.shape[0] - EXTRA
    for own, got, out, start in ((for_right, right, right_out, 0), (for_left, left, left_out, count - arrived)):
        if arrived < count:
            out[:count] = own[0, :count]
        spot = slice(start, start + arrived)
        out[spot] = (own[0, spot].astype(F32) + got[:arrived].astype(F32)).astype(BF)
        out[count:] = jnp.concatenate([own[0, count:, :128], got[arrived:, :-128]], axis=1)


def forward(shares, at, right, left):
    depth, rows, lanes = shares.shape
    shape = jax.ShapeDtypeStruct((rows, lanes), BF)
    return pl.pallas_call(
        forward_kernel,
        grid=(1,),
        in_specs=[
            pl.BlockSpec((1, rows, lanes), lambda _: (at, 0, 0)),
            pl.BlockSpec((1, rows, lanes), lambda _: (depth - at, 0, 0)),
            whole(right.shape),
            whole(left.shape),
        ],
        out_specs=[whole((rows, lanes))] * 2,
        out_shape=[shape, shape],
        compiler_params=params(VMEM_SOME),
    )(shares, shares, right, left)


def final_kernel(regions, full, depth, me, back, own, right, left, tok, gain, routes, weights, moe_out, grad_out, comb_out, stack):
    count = tok.shape[0]
    late = tok.shape[1] - EARLY
    high, low = combining(routes[...], weights[...], regions)
    moe, grad = [dot(high, rows, TN) + dot(low, rows, TN) for rows in decode(back[...], late, fold_matrix(regions))]
    early = own[0, :count].astype(F32) + right[:count].astype(F32) + left[:count].astype(F32)
    moe_out[:, :late] = moe.astype(BF)
    moe_out[:, late:] = early[:, :EARLY].astype(BF)
    wide = tok[...].astype(F32)
    stack[0] = own[0, count:, :count].astype(F32)
    for away in range(1, depth):
        source, slot = (left, away - 1) if away <= depth // 2 else (right, depth - away - 1)
        stack[away] = source[count:, slot * 128 : slot * 128 + count].astype(F32)
    total = 0.0
    for z in range(depth):
        total = total + stack[(z - me[0] + depth) % depth]
    comb = [total[3 * k : 3 * k + 1] + total[3 * k + 1 : 3 * k + 2] + total[3 * k + 2 : 3 * k + 3] for k in range(3)]
    comb_out[0:1] = comb[0]
    comb_out[1:2] = comb[1]
    inv = inverse(total[9:10] + total[10:11] + total[11:12], full)
    row = lax.broadcasted_iota(jnp.int32, (8, count), 0)
    columns = jnp.transpose(jnp.where(row == 0, comb[2], jnp.where(row == 1, inv, 0.0)))
    inner, inv = columns[:, 0:1], columns[:, 1:2]
    scaled = gain[...].reshape(1, -1) * jnp.concatenate([grad, early[:, EARLY:]], axis=1)
    grad_out[...] = (inv * scaled - wide * (inv * inv * inv * inner / full)).astype(BF)


def final(me, back, shares, right, left, tok, gain, routes, weights, regions, full):
    count, width = tok.shape
    depth, rows, lanes = shares.shape
    shapes = [
        jax.ShapeDtypeStruct((count, width), BF),
        jax.ShapeDtypeStruct((count, width), BF),
        jax.ShapeDtypeStruct((2, count), F32),
    ]
    operands = (back, shares, right, left, tok, gain, routes, weights)
    specs = [whole(operand.shape) for operand in operands]
    specs[1] = pl.BlockSpec((1, rows, lanes), lambda *_: (0, 0, 0))
    return pl.pallas_call(
        functools.partial(final_kernel, regions, full, depth),
        grid_spec=pltpu.PrefetchScalarGridSpec(
            num_scalar_prefetch=1,
            grid=(1,),
            in_specs=specs,
            out_specs=[whole(shape.shape) for shape in shapes],
            scratch_shapes=[pltpu.VMEM((depth, EXTRA, count), F32)],
        ),
        out_shape=shapes,
        compiler_params=params(VMEM_SOME),
    )(me, *operands)


def swap(array, regions):
    split = array.reshape(regions, 8, array.shape[1])
    moved = lax.all_to_all(split, "region", split_axis=0, concat_axis=0, tiled=True)
    return moved.reshape(array.shape)


def hop(array, step):
    depth = lax.axis_size("local")
    return lax.ppermute(array, "local", [(z, (z + step) % depth) for z in range(depth)])


def ring_gather(own):
    half = lax.axis_size("local") // 2
    low, high = own, own
    blocks = [own]
    for _ in range(half - 1):
        low, high = lax.optimization_barrier((hop(low, 1), hop(high, -1)))
        blocks += [low, high]
    cut = (own.shape[0] - EXTRA) // 2
    return blocks + [hop(low[:cut], 1), hop(high[cut:], -1)]


def ring_scatter(shares, right, left):
    for at in range(shares.shape[0] // 2 - 1, -1, -1):
        right, left = hop(right, 1), hop(left, -1)
        if at:
            right, left = forward(shares, at, right, left)
    return right, left


def on_device(tokens, norm_gain, w_gate, w_up, w_down, routes, combine, grad_out):
    regions = lax.axis_size("region")
    depth = lax.axis_size("local")
    me = lax.axis_index("local").astype(jnp.int32).reshape(1)
    full = depth * tokens.shape[1]
    gain = norm_gain
    routes, weights = routes.T, combine.T
    packed, early = pack(tokens, gain, grad_out, routes, regions)
    around = ring_gather(early)
    arrived, _ = lax.optimization_barrier((swap(packed, regions), around[4]))
    blocks = lax.all_gather(arrived, "local")
    early_rows = pack_early(around, routes, regions, depth, full)
    rows = swap(early_rows, regions)
    partial, back_rows = expert_part(me, blocks, rows, w_gate, w_up, w_down, regions)
    summed = lax.psum_scatter(partial, "local", scatter_dimension=0)
    shares, right, left = combine_early(early, swap(back_rows, regions), routes, weights, regions, depth)
    right, left = ring_scatter(shares, right, left)
    moe, grad, comb = final(me, swap(summed, regions), shares, right, left, tokens, gain, routes, weights, regions, full)
    return moe, grad, comb.T


def solution(mesh):
    specs = (
        P("region", "local"),
        P("local"),
        P("region", None, "local"),
        P("region", None, "local"),
        P("region", "local", None),
        P("region", None),
        P("region", None),
        P("region", "local"),
    )
    return jax.shard_map(
        on_device,
        mesh=mesh,
        in_specs=specs,
        out_specs=(P("region", "local"), P("region", "local"), P("region", None)),
        check_vma=False,
    )
```

```python
import functools

import jax
import jax.numpy as jnp
from jax import lax
from jax.experimental import pallas as pl
from jax.experimental.pallas import tpu as pltpu
from jax.sharding import PartitionSpec as P

BF = jnp.bfloat16
F32 = jnp.float32
NT = (((1,), (1,)), ((), ()))
TN = (((0,), (0,)), ((), ()))
VMEM_MOST = 63 * 1024 * 1024
VMEM_SOME = 40 * 1024 * 1024
EXTRA = 16
EARLY = (384, 256)
EARLY_LANES = sum(EARLY)


def late_widths(width):
    return [width - early for early in EARLY]


def fold_lanes(widths):
    return max(128 * -(-width // 256) for width in widths)


def packed_lanes(widths):
    return sum(widths) + fold_lanes(widths)


def dot(a, b, dims=(((1,), (0,)), ((), ())), precision=None):
    return lax.dot_general(a, b, dims, precision=precision, preferred_element_type=F32)


def params(limit=VMEM_MOST):
    return pltpu.CompilerParams(vmem_limit_bytes=limit)


def whole(shape):
    return pl.BlockSpec(shape, lambda *_: (0,) * len(shape))


def fold_matrix(regions):
    rows = 8 * regions
    i = lax.broadcasted_iota(jnp.int32, (rows, rows), 0)
    j = lax.broadcasted_iota(jnp.int32, (rows, rows), 1)
    return (j == 4 * (i % (2 * regions)) + i // (2 * regions)).astype(BF)


def encode(main, rest, fold, widths):
    lanes = fold_lanes(widths)
    parts = []
    start = 0
    for width in widths:
        parts.append(rest[:, start : start + lanes])
        tail = rest[:, start + lanes : start + width]
        pad = 2 * lanes - width
        if pad:
            tail = jnp.concatenate([tail, jnp.zeros((rest.shape[0], pad), rest.dtype)], axis=1)
        parts.append(tail)
        start += width
    stacked = jnp.concatenate(parts, axis=0)
    return jnp.concatenate([main, dot(fold, stacked, TN).astype(BF)], axis=1)


def decode(block, widths, fold):
    lanes = fold_lanes(widths)
    few = block.shape[0] // 4
    rest = dot(fold, block[:, sum(widths) :]).astype(BF)
    sides = []
    start = 0
    for side, width in enumerate(widths):
        head = rest[(2 * side) * few : (2 * side + 1) * few]
        tail = rest[(2 * side + 1) * few : (2 * side + 2) * few, : width - lanes]
        low = jnp.concatenate([head, tail], axis=1)
        sides.append(jnp.concatenate([block[:, start : start + width], low], axis=0))
        start += width
    return sides


def slot_ids(regions, tokens):
    s = lax.broadcasted_iota(jnp.int32, (10 * regions, tokens), 0)
    late = s - 8 * regions
    expert = jnp.where(late < 0, s // 8, late // 2)
    slot = jnp.where(late < 0, s % 8, 8 + late % 2)
    return expert, slot


def ranks(named):
    count = named.shape[1]
    before = lax.broadcasted_iota(jnp.int32, (count, count), 0)
    after = lax.broadcasted_iota(jnp.int32, (count, count), 1)
    return dot(named.astype(F32).astype(BF), (before < after).astype(F32).astype(BF))


def placed(routes, regions):
    expert, slot = slot_ids(regions, routes.shape[1])
    named = [routes[k : k + 1, :] == expert for k in range(2)]
    at = ranks(named[0] | named[1]) == slot.astype(F32)
    return [n & at for n in named]


def placed_packed(routes, regions):
    s = lax.broadcasted_iota(jnp.int32, (8 * regions, routes.shape[1]), 0)
    expert = s // 8
    named = [routes[k : k + 1, :] == expert for k in range(2)]
    rank = ranks(named[0] | named[1])
    main = rank == (s % 8).astype(F32)
    late = (rank == (8 + (s % 8) // 4).astype(F32)) & (s % 4 == 0)
    return [n & main for n in named], [n & late for n in named]


def once(kernel, out_shape, *operands, limit=VMEM_SOME):
    many = isinstance(out_shape, list)
    specs = [whole(shape.shape) for shape in (out_shape if many else [out_shape])]
    return pl.pallas_call(
        kernel,
        grid=(1,),
        in_specs=[whole(operand.shape) for operand in operands],
        out_specs=specs if many else specs[0],
        out_shape=out_shape,
        compiler_params=params(limit),
    )(*operands)


def triple(value):
    high = value.astype(BF)
    value = value - high.astype(F32)
    middle = value.astype(BF)
    return [high, middle, (value - middle.astype(F32)).astype(BF)]


def in_lanes(columns, rows):
    lane = lax.broadcasted_iota(jnp.int32, (rows, 128), 1)
    out = jnp.zeros((rows, 128), F32)
    for at, column in enumerate(columns):
        if column is not None:
            out = jnp.where(lane == at, column.astype(F32), out)
    return out.astype(BF)


def from_lanes(block, at):
    block = block.astype(F32)
    return block[:, at : at + 1] + block[:, at + 1 : at + 2] + block[:, at + 2 : at + 3]


def in_rows(rows, lanes):
    count = rows[0].shape[1]
    row = lax.broadcasted_iota(jnp.int32, (EXTRA, count), 0)
    out = jnp.zeros((EXTRA, count), F32)
    for at, value in enumerate(rows):
        out = jnp.where(row == at, value.astype(F32), out)
    out = out.astype(BF)
    return jnp.concatenate([out, jnp.zeros((EXTRA, lanes - count), BF)], axis=1)


def pack_kernel(regions, tok, gain, grad, routes, out, early):
    at = placed(routes[...], regions)
    pick = (at[0] | at[1]).astype(F32).astype(BF)
    late = late_widths(tok.shape[1])
    count = tok.shape[0]
    wide = tok[...].astype(F32)
    scaled = (wide * gain[...].reshape(1, -1)).astype(BF)
    rows = dot(pick, jnp.concatenate([scaled[:, : late[0]], grad[:, : late[1]]], axis=1)).astype(BF)
    cut = 8 * regions
    out[...] = encode(rows[:cut], rows[cut:], fold_matrix(regions), late)
    early[:count] = jnp.concatenate([scaled[:, late[0] :], grad[:, late[1] :]], axis=1)
    squares = jnp.broadcast_to(jnp.sum(wide * wide, axis=1, keepdims=True), (count, 128))
    early[count:] = in_rows(triple(jnp.transpose(squares)[0:1]), early.shape[1])


def pack(tok, gain, grad, routes, regions):
    count, width = tok.shape
    shapes = [
        jax.ShapeDtypeStruct((8 * regions, packed_lanes(late_widths(width))), BF),
        jax.ShapeDtypeStruct((count + EXTRA, EARLY_LANES), BF),
    ]
    return once(functools.partial(pack_kernel, regions), shapes, tok, gain, grad, routes, limit=VMEM_MOST)


def inverse(squares, full):
    return lax.rsqrt(squares / full + 1e-06)


def pack_early_kernel(regions, depth, full, routes, *refs):
    blocks, out = refs[:-1], refs[-1]
    lanes = blocks[0].shape[1]
    early = {0: blocks[0][...]}
    half = depth // 2
    for hop in range(1, half):
        early[depth - hop] = blocks[2 * hop - 1][...]
        early[hop] = blocks[2 * hop][...]
    early[half] = jnp.concatenate([blocks[-2][...], blocks[-1][...]], axis=0)
    at = placed(routes[...], regions)
    pick = (at[0] | at[1]).astype(F32).astype(BF)
    cut = 8 * regions
    rests = []
    count = routes.shape[1]
    squares = 0.0
    for z in range(depth):
        rows = dot(pick, early[z][:count]).astype(BF)
        extra = early[z][count:, :count].astype(F32)
        squares = squares + extra[0:1] + extra[1:2] + extra[2:3]
        out[:, z * lanes : (z + 1) * lanes] = rows[:cut]
        rests.append(rows[cut:])
    for half in range(depth // 4):
        stacked = jnp.concatenate(rests[4 * half : 4 * half + 4], axis=0)
        at_lane = (depth + half) * lanes
        out[:, at_lane : at_lane + lanes] = dot(fold_matrix(regions), stacked, TN).astype(BF)
    inv = inverse(squares, full)
    columns = []
    for found in placed_packed(routes[...], regions):
        columns += triple(jnp.sum(jnp.where(found[0] | found[1], inv, 0.0), axis=1, keepdims=True))
    out[:, -128:] = in_lanes(columns, cut)


def early_shape(regions, depth):
    return (8 * regions, EARLY_LANES * depth * 5 // 4 + 128)


def pack_early(blocks, routes, regions, depth, full):
    shape = jax.ShapeDtypeStruct(early_shape(regions, depth), BF)
    return once(functools.partial(pack_early_kernel, regions, depth, full), shape, routes, *blocks)


def anywhere():
    return pl.BlockSpec(memory_space=pl.ANY)


def expert_kernel(
    regions,
    depth,
    me,
    blocks,
    rows,
    gate_hbm,
    up_hbm,
    down_hbm,
    late_out,
    early_out,
    gate_w,
    up_w,
    down_w,
    acc_g,
    acc_u,
    acc_h,
    hid,
    gate_g,
    up_g,
    scal,
    fold,
    scales,
    sem,
    weight_sems,
):
    width = gate_w.shape[1] // depth
    few = 2 * regions
    cut, lanes = blocks.shape[1:]
    late = late_widths(width)
    first_block = me[0]
    copy = pltpu.make_async_copy(rows.at[:, rows.shape[1] - 128 :], scales, sem)
    copy.start()

    def lanes_of(step):
        return pl.ds(pl.multiple_of((step + first_block) % depth * width, 128), width)

    def weight_copies(step):
        at = lanes_of(step)
        return [
            pltpu.make_async_copy(gate_hbm.at[:, at, :], gate_w.at[:, at, :], weight_sems.at[0, step]),
            pltpu.make_async_copy(up_hbm.at[:, at, :], up_w.at[:, at, :], weight_sems.at[1, step]),
            pltpu.make_async_copy(down_hbm.at[:, :, at], down_w.at[:, :, at], weight_sems.at[2, step]),
        ]

    for step in range(depth):
        for one in weight_copies(step):
            one.start()
    fold[...] = fold_matrix(regions)
    acc_g[...] = jnp.zeros_like(acc_g)
    acc_u[...] = jnp.zeros_like(acc_u)
    acc_h[...] = jnp.zeros_like(acc_h)

    def body(block, main, rest):
        step = pl.program_id(0)
        at = lanes_of(step)
        for one in weight_copies(step):
            one.wait()
        late_in, late_grad = decode(block[0], late, fold[...])
        pick = fold[pl.ds(pl.multiple_of((step % 4) * few, few), few), :]
        early = jnp.concatenate([main[...], dot(pick, rest[...]).astype(BF)], axis=0)
        rows_in = jnp.concatenate([late_in, early[:, : EARLY[0]]], axis=1)
        rows_grad = jnp.concatenate([late_grad, early[:, EARLY[0] :]], axis=1)
        acc_g[...] += dot(rows_in, gate_w[0, at, :])
        acc_u[...] += dot(rows_in, up_w[0, at, :])
        acc_h[...] += dot(rows_grad, down_w[0, :, at], NT)

    pltpu.emit_pipeline(
        body,
        grid=(depth,),
        in_specs=[
            pl.BlockSpec((1, cut, lanes), lambda z: ((z + first_block) % depth, 0, 0)),
            pl.BlockSpec((cut, EARLY_LANES), lambda z: (0, z)),
            pl.BlockSpec((cut, EARLY_LANES), lambda z: (0, depth + z // 4)),
        ],
    )(blocks, rows, rows)

    copy.wait()
    first = fold[0:few, :]
    inv = jnp.concatenate([from_lanes(scales[...], 0), from_lanes(dot(first, scales[...]), 3)], axis=0)
    gate_raw, up_raw, grad_hidden = acc_g[...], acc_u[...], acc_h[...]
    gate_pre, up_pre = gate_raw * inv, up_raw * inv
    sig = jax.nn.sigmoid(gate_pre)
    act = gate_pre * sig
    hidden = (act * up_pre).astype(BF)
    grad_gate = (grad_hidden * up_pre * sig * (1.0 + gate_pre * (1.0 - sig))).astype(BF)
    grad_up = (grad_hidden * act).astype(BF)
    hid[...] = hidden
    gate_g[...] = grad_gate
    up_g[...] = grad_up
    comb = jnp.sum(hidden.astype(F32) * grad_hidden, axis=1, keepdims=True)
    inner = jnp.sum(grad_gate.astype(F32) * gate_raw + grad_up.astype(F32) * up_raw, axis=1, keepdims=True)
    here = in_lanes(triple(comb[:cut]) + triple(inner[:cut]), cut)
    there = in_lanes([None] * 6 + triple(comb[cut:]) + triple(inner[cut:]), few)
    scal[...] = here + dot(first, there, TN).astype(BF)
    late_lanes = late_out.shape[2]

    def back(late_block, main, rest):
        step = pl.program_id(0)
        at = lanes_of(step)
        moe = dot(hid[...], down_w[0, :, at]).astype(BF)
        grad = (dot(gate_g[...], gate_w[0, at, :], NT) + dot(up_g[...], up_w[0, at, :], NT)).astype(BF)
        both = jnp.concatenate([moe[:, : late[0]], grad[:, : late[1]]], axis=1)
        late_block[0] = encode(both[:cut], both[cut:], fold[...], late)
        both = jnp.concatenate([moe[:, late[0] :], grad[:, late[1] :]], axis=1)
        main[...] = both[:cut]
        pick = fold[pl.ds(pl.multiple_of((step % 4) * few, few), few), :]
        low = dot(pick, both[cut:], TN).astype(BF)

        @pl.when(step % 4 == 0)
        def _():
            rest[...] = low

        @pl.when(step % 4 > 0)
        def _():
            rest[...] = rest[...] + low

    pltpu.emit_pipeline(
        back,
        grid=(depth,),
        out_specs=[
            pl.BlockSpec((1, cut, late_lanes), lambda z: ((z + first_block) % depth, 0, 0)),
            pl.BlockSpec((cut, EARLY_LANES), lambda z: (0, z)),
            pl.BlockSpec((cut, EARLY_LANES), lambda z: (0, depth + z // 4)),
        ],
    )(late_out, early_out, early_out)
    pltpu.sync_copy(scal, early_out.at[:, early_out.shape[1] - 128 :])


def expert_part(me, blocks, rows, gate_w, up_w, down_w, regions):
    depth, cut, lanes = blocks.shape
    units = gate_w.shape[2]
    total = 10 * regions
    return pl.pallas_call(
        functools.partial(expert_kernel, regions, depth),
        in_specs=[pl.BlockSpec(memory_space=pltpu.SMEM)] + [anywhere()] * 5,
        out_specs=[anywhere()] * 2,
        out_shape=[jax.ShapeDtypeStruct((depth, cut, lanes), BF), jax.ShapeDtypeStruct(rows.shape, BF)],
        scratch_shapes=[pltpu.VMEM(w.shape, BF) for w in (gate_w, up_w, down_w)]
        + [pltpu.VMEM((total, units), F32)] * 3
        + [pltpu.VMEM((total, units), BF)] * 3
        + [pltpu.VMEM((cut, 128), BF), pltpu.VMEM((cut, cut), BF), pltpu.VMEM((cut, 128), BF)]
        + [pltpu.SemaphoreType.DMA(()), pltpu.SemaphoreType.DMA((3, depth))],
        compiler_params=params(VMEM_MOST),
    )(me, blocks, rows, gate_w, up_w, down_w)


def scalars(here, routes, weights, regions):
    main, late = placed_packed(routes, regions)
    parts = []
    inner = 0.0
    for k in range(2):
        comb = jnp.where(main[k], from_lanes(here, 0), 0.0) + jnp.where(late[k], from_lanes(here, 6), 0.0)
        part = jnp.where(main[k], from_lanes(here, 3), 0.0) + jnp.where(late[k], from_lanes(here, 9), 0.0)
        parts.append(jnp.sum(comb, axis=0, keepdims=True))
        inner = inner + weights[k : k + 1, :] * jnp.sum(part, axis=0, keepdims=True)
    return parts + [inner]


def combining(routes, weights, regions):
    at = placed(routes, regions)
    weight = jnp.where(at[0], weights[0:1, :], 0.0) + jnp.where(at[1], weights[1:2, :], 0.0)
    high = weight.astype(BF)
    return high, (weight - high.astype(F32)).astype(BF)


def combine_early_kernel(regions, squares, back, routes, weights, out, right, left):
    depth, rows_out, lanes = out.shape
    count = rows_out - EXTRA
    high, low = combining(routes[...], weights[...], regions)
    quarter = depth // 4
    few = 2 * regions
    values = []
    for value in scalars(back[:, -128:], routes[...], weights[...], regions):
        values += triple(value)
    count = routes.shape[1]
    values += [squares[at : at + 1, :count] for at in range(3)]
    extra = in_rows(values, lanes)
    fold = fold_matrix(regions)
    rests = [dot(fold, back[:, (depth + half) * lanes : (depth + half + 1) * lanes]).astype(BF) for half in range(quarter)]
    for z in range(depth):
        part = z % 4
        rest = rests[z // 4][part * few : (part + 1) * few]
        rows = jnp.concatenate([back[:, z * lanes : (z + 1) * lanes], rest], axis=0)
        share = (dot(high, rows, TN) + dot(low, rows, TN)).astype(BF)
        out[z, :count] = share
        out[z, count:] = extra
        if z == depth // 2:
            right[...] = jnp.concatenate([share[: count // 2], extra], axis=0)
            left[...] = jnp.concatenate([share[count // 2 :], extra], axis=0)


def combine_early(early, back, routes, weights, regions, depth):
    count = routes.shape[1]
    squares = early[count:]
    lanes = EARLY_LANES
    shapes = [
        jax.ShapeDtypeStruct((depth, count + EXTRA, lanes), BF),
        jax.ShapeDtypeStruct((count // 2 + EXTRA, lanes), BF),
        jax.ShapeDtypeStruct((count // 2 + EXTRA, lanes), BF),
    ]
    return once(functools.partial(combine_early_kernel, regions), shapes, squares, back, routes, weights, limit=VMEM_MOST)


def forward_kernel(for_right, for_left, right, left, right_out, left_out):
    rows = for_right.shape[1]
    count = rows - EXTRA
    arrived = right.shape[0] - EXTRA
    for own, got, out, start in ((for_right, right, right_out, 0), (for_left, left, left_out, count - arrived)):
        if arrived < count:
            out[:count] = own[0, :count]
        spot = slice(start, start + arrived)
        out[spot] = (own[0, spot].astype(F32) + got[:arrived].astype(F32)).astype(BF)
        out[count:] = jnp.concatenate([own[0, count:, :128], got[arrived:, :-128]], axis=1)


def forward(shares, at, right, left):
    depth, rows, lanes = shares.shape
    shape = jax.ShapeDtypeStruct((rows, lanes), BF)
    return pl.pallas_call(
        forward_kernel,
        grid=(1,),
        in_specs=[
            pl.BlockSpec((1, rows, lanes), lambda _: (at, 0, 0)),
            pl.BlockSpec((1, rows, lanes), lambda _: (depth - at, 0, 0)),
            whole(right.shape),
            whole(left.shape),
        ],
        out_specs=[whole((rows, lanes))] * 2,
        out_shape=[shape, shape],
        compiler_params=params(VMEM_SOME),
    )(shares, shares, right, left)


def final_kernel(regions, full, depth, me, back, own, right, left, tok, gain, routes, weights, moe_out, grad_out, comb_out, stack):
    count = tok.shape[0]
    late = late_widths(tok.shape[1])
    high, low = combining(routes[...], weights[...], regions)
    moe, grad = [dot(high, rows, TN) + dot(low, rows, TN) for rows in decode(back[...], late, fold_matrix(regions))]
    early = own[0, :count].astype(F32) + right[:count].astype(F32) + left[:count].astype(F32)
    moe_out[:, : late[0]] = moe.astype(BF)
    moe_out[:, late[0] :] = early[:, : EARLY[0]].astype(BF)
    wide = tok[...].astype(F32)
    stack[0] = own[0, count:, :count].astype(F32)
    for away in range(1, depth):
        source, slot = (left, away - 1) if away <= depth // 2 else (right, depth - away - 1)
        stack[away] = source[count:, slot * 128 : slot * 128 + count].astype(F32)
    total = 0.0
    for z in range(depth):
        total = total + stack[(z - me[0] + depth) % depth]
    comb = [total[3 * k : 3 * k + 1] + total[3 * k + 1 : 3 * k + 2] + total[3 * k + 2 : 3 * k + 3] for k in range(3)]
    comb_out[0:1] = comb[0]
    comb_out[1:2] = comb[1]
    inv = inverse(total[9:10] + total[10:11] + total[11:12], full)
    row = lax.broadcasted_iota(jnp.int32, (8, count), 0)
    columns = jnp.transpose(jnp.where(row == 0, comb[2], jnp.where(row == 1, inv, 0.0)))
    inner, inv = columns[:, 0:1], columns[:, 1:2]
    scaled = gain[...].reshape(1, -1) * jnp.concatenate([grad, early[:, EARLY[0] :]], axis=1)
    grad_out[...] = (inv * scaled - wide * (inv * inv * inv * inner / full)).astype(BF)


def final(me, back, shares, right, left, tok, gain, routes, weights, regions, full):
    count, width = tok.shape
    depth, rows, lanes = shares.shape
    shapes = [
        jax.ShapeDtypeStruct((count, width), BF),
        jax.ShapeDtypeStruct((count, width), BF),
        jax.ShapeDtypeStruct((2, count), F32),
    ]
    operands = (back, shares, right, left, tok, gain, routes, weights)
    specs = [whole(operand.shape) for operand in operands]
    specs[1] = pl.BlockSpec((1, rows, lanes), lambda *_: (0, 0, 0))
    return pl.pallas_call(
        functools.partial(final_kernel, regions, full, depth),
        grid_spec=pltpu.PrefetchScalarGridSpec(
            num_scalar_prefetch=1,
            grid=(1,),
            in_specs=specs,
            out_specs=[whole(shape.shape) for shape in shapes],
            scratch_shapes=[pltpu.VMEM((depth, EXTRA, count), F32)],
        ),
        out_shape=shapes,
        compiler_params=params(VMEM_SOME),
    )(me, *operands)


def swap(array, regions):
    split = array.reshape(regions, 8, array.shape[1])
    moved = lax.all_to_all(split, "region", split_axis=0, concat_axis=0, tiled=True)
    return moved.reshape(array.shape)


def hop(array, step):
    depth = lax.axis_size("local")
    return lax.ppermute(array, "local", [(z, (z + step) % depth) for z in range(depth)])


def ring_gather(own):
    half = lax.axis_size("local") // 2
    low, high = own, own
    blocks = [own]
    for _ in range(half - 1):
        low, high = lax.optimization_barrier((hop(low, 1), hop(high, -1)))
        blocks += [low, high]
    cut = (own.shape[0] - EXTRA) // 2
    return blocks + [hop(low[:cut], 1), hop(high[cut:], -1)]


def ring_scatter(shares, right, left, summed):
    for at in range(shares.shape[0] // 2 - 1, -1, -1):
        right, left = hop(right, 1), hop(left, -1)
        if at == shares.shape[0] // 2 - 2:
            summed, _, _ = lax.optimization_barrier((summed, right, left))
        if at:
            right, left = forward(shares, at, right, left)
    return right, left, summed


def on_device(tokens, norm_gain, w_gate, w_up, w_down, routes, combine, grad_out):
    regions = lax.axis_size("region")
    depth = lax.axis_size("local")
    me = lax.axis_index("local").astype(jnp.int32).reshape(1)
    full = depth * tokens.shape[1]
    gain = norm_gain
    routes, weights = routes.T, combine.T
    packed, early = pack(tokens, gain, grad_out, routes, regions)
    around = ring_gather(early)
    arrived, _ = lax.optimization_barrier((swap(packed, regions), around[4]))
    blocks = lax.all_gather(arrived, "local")
    early_rows = pack_early(around, routes, regions, depth, full)
    rows = swap(early_rows, regions)
    partial, back_rows = expert_part(me, blocks, rows, w_gate, w_up, w_down, regions)
    summed = lax.psum_scatter(partial, "local", scatter_dimension=0)
    shares, right, left = combine_early(early, swap(back_rows, regions), routes, weights, regions, depth)
    right, left, summed = ring_scatter(shares, right, left, summed)
    moe, grad, comb = final(me, swap(summed, regions), shares, right, left, tokens, gain, routes, weights, regions, full)
    return moe, grad, comb.T


def solution(mesh):
    specs = (
        P("region", "local"),
        P("local"),
        P("region", None, "local"),
        P("region", None, "local"),
        P("region", "local", None),
        P("region", None),
        P("region", None),
        P("region", "local"),
    )
    return jax.shard_map(
        on_device,
        mesh=mesh,
        in_specs=specs,
        out_specs=(P("region", "local"), P("region", "local"), P("region", None)),
        check_vma=False,
    )
```

```python
import functools

import jax
import jax.numpy as jnp
from jax import lax
from jax.experimental import pallas as pl
from jax.experimental.pallas import tpu as pltpu
from jax.sharding import PartitionSpec as P

BF = jnp.bfloat16
F32 = jnp.float32
NT = (((1,), (1,)), ((), ()))
TN = (((0,), (0,)), ((), ()))
VMEM_MOST = 63 * 1024 * 1024
VMEM_SOME = 40 * 1024 * 1024
EXTRA = 16
EARLY = (384, 256)
BACK = (384, 384)


def late_widths(width, early):
    return [width - lanes for lanes in early]


def fold_lanes(widths):
    return max(128 * -(-width // 256) for width in widths)


def packed_lanes(widths):
    return sum(widths) + fold_lanes(widths)


def dot(a, b, dims=(((1,), (0,)), ((), ())), precision=None):
    return lax.dot_general(a, b, dims, precision=precision, preferred_element_type=F32)


def params(limit=VMEM_MOST):
    return pltpu.CompilerParams(vmem_limit_bytes=limit)


def whole(shape):
    return pl.BlockSpec(shape, lambda *_: (0,) * len(shape))


def fold_matrix(regions):
    rows = 8 * regions
    i = lax.broadcasted_iota(jnp.int32, (rows, rows), 0)
    j = lax.broadcasted_iota(jnp.int32, (rows, rows), 1)
    return (j == 4 * (i % (2 * regions)) + i // (2 * regions)).astype(BF)


def encode(main, rest, fold, widths):
    lanes = fold_lanes(widths)
    parts = []
    start = 0
    for width in widths:
        parts.append(rest[:, start : start + lanes])
        tail = rest[:, start + lanes : start + width]
        pad = 2 * lanes - width
        if pad:
            tail = jnp.concatenate([tail, jnp.zeros((rest.shape[0], pad), rest.dtype)], axis=1)
        parts.append(tail)
        start += width
    stacked = jnp.concatenate(parts, axis=0)
    return jnp.concatenate([main, dot(fold, stacked, TN).astype(BF)], axis=1)


def decode(block, widths, fold):
    lanes = fold_lanes(widths)
    few = block.shape[0] // 4
    rest = dot(fold, block[:, sum(widths) :]).astype(BF)
    sides = []
    start = 0
    for side, width in enumerate(widths):
        head = rest[(2 * side) * few : (2 * side + 1) * few]
        tail = rest[(2 * side + 1) * few : (2 * side + 2) * few, : width - lanes]
        low = jnp.concatenate([head, tail], axis=1)
        sides.append(jnp.concatenate([block[:, start : start + width], low], axis=0))
        start += width
    return sides


def slot_ids(regions, tokens):
    s = lax.broadcasted_iota(jnp.int32, (10 * regions, tokens), 0)
    late = s - 8 * regions
    expert = jnp.where(late < 0, s // 8, late // 2)
    slot = jnp.where(late < 0, s % 8, 8 + late % 2)
    return expert, slot


def ranks(named):
    count = named.shape[1]
    before = lax.broadcasted_iota(jnp.int32, (count, count), 0)
    after = lax.broadcasted_iota(jnp.int32, (count, count), 1)
    return dot(named.astype(F32).astype(BF), (before < after).astype(F32).astype(BF))


def placed(routes, regions):
    expert, slot = slot_ids(regions, routes.shape[1])
    named = [routes[k : k + 1, :] == expert for k in range(2)]
    at = ranks(named[0] | named[1]) == slot.astype(F32)
    return [n & at for n in named]


def placed_packed(routes, regions):
    s = lax.broadcasted_iota(jnp.int32, (8 * regions, routes.shape[1]), 0)
    expert = s // 8
    named = [routes[k : k + 1, :] == expert for k in range(2)]
    rank = ranks(named[0] | named[1])
    main = rank == (s % 8).astype(F32)
    late = (rank == (8 + (s % 8) // 4).astype(F32)) & (s % 4 == 0)
    return [n & main for n in named], [n & late for n in named]


def once(kernel, out_shape, *operands, limit=VMEM_SOME):
    many = isinstance(out_shape, list)
    specs = [whole(shape.shape) for shape in (out_shape if many else [out_shape])]
    return pl.pallas_call(
        kernel,
        grid=(1,),
        in_specs=[whole(operand.shape) for operand in operands],
        out_specs=specs if many else specs[0],
        out_shape=out_shape,
        compiler_params=params(limit),
    )(*operands)


def triple(value):
    high = value.astype(BF)
    value = value - high.astype(F32)
    middle = value.astype(BF)
    return [high, middle, (value - middle.astype(F32)).astype(BF)]


def in_lanes(columns, rows):
    lane = lax.broadcasted_iota(jnp.int32, (rows, 128), 1)
    out = jnp.zeros((rows, 128), F32)
    for at, column in enumerate(columns):
        if column is not None:
            out = jnp.where(lane == at, column.astype(F32), out)
    return out.astype(BF)


def from_lanes(block, at):
    block = block.astype(F32)
    return block[:, at : at + 1] + block[:, at + 1 : at + 2] + block[:, at + 2 : at + 3]


def in_rows(rows, lanes):
    count = rows[0].shape[1]
    row = lax.broadcasted_iota(jnp.int32, (EXTRA, count), 0)
    out = jnp.zeros((EXTRA, count), F32)
    for at, value in enumerate(rows):
        out = jnp.where(row == at, value.astype(F32), out)
    out = out.astype(BF)
    return jnp.concatenate([out, jnp.zeros((EXTRA, lanes - count), BF)], axis=1)


def pack_kernel(regions, tok, gain, grad, routes, out, early):
    at = placed(routes[...], regions)
    pick = (at[0] | at[1]).astype(F32).astype(BF)
    late = late_widths(tok.shape[1], EARLY)
    count = tok.shape[0]
    wide = tok[...].astype(F32)
    scaled = (wide * gain[...].reshape(1, -1)).astype(BF)
    rows = dot(pick, jnp.concatenate([scaled[:, : late[0]], grad[:, : late[1]]], axis=1)).astype(BF)
    cut = 8 * regions
    out[...] = encode(rows[:cut], rows[cut:], fold_matrix(regions), late)
    early[:count] = jnp.concatenate([scaled[:, late[0] :], grad[:, late[1] :]], axis=1)
    squares = jnp.broadcast_to(jnp.sum(wide * wide, axis=1, keepdims=True), (count, 128))
    early[count:] = in_rows(triple(jnp.transpose(squares)[0:1]), early.shape[1])


def pack(tok, gain, grad, routes, regions):
    count, width = tok.shape
    shapes = [
        jax.ShapeDtypeStruct((8 * regions, packed_lanes(late_widths(width, EARLY))), BF),
        jax.ShapeDtypeStruct((count + EXTRA, sum(EARLY)), BF),
    ]
    return once(functools.partial(pack_kernel, regions), shapes, tok, gain, grad, routes, limit=VMEM_MOST)


def inverse(squares, full):
    return lax.rsqrt(squares / full + 1e-06)


def pack_early_kernel(regions, depth, full, routes, *refs):
    blocks, out = refs[:-1], refs[-1]
    lanes = blocks[0].shape[1]
    early = {0: blocks[0][...]}
    half = depth // 2
    for hop in range(1, half):
        early[depth - hop] = blocks[2 * hop - 1][...]
        early[hop] = blocks[2 * hop][...]
    early[half] = jnp.concatenate([blocks[-2][...], blocks[-1][...]], axis=0)
    at = placed(routes[...], regions)
    pick = (at[0] | at[1]).astype(F32).astype(BF)
    cut = 8 * regions
    rests = []
    count = routes.shape[1]
    squares = 0.0
    for z in range(depth):
        rows = dot(pick, early[z][:count]).astype(BF)
        extra = early[z][count:, :count].astype(F32)
        squares = squares + extra[0:1] + extra[1:2] + extra[2:3]
        out[:, z * lanes : (z + 1) * lanes] = rows[:cut]
        rests.append(rows[cut:])
    for half in range(depth // 4):
        stacked = jnp.concatenate(rests[4 * half : 4 * half + 4], axis=0)
        at_lane = (depth + half) * lanes
        out[:, at_lane : at_lane + lanes] = dot(fold_matrix(regions), stacked, TN).astype(BF)
    inv = inverse(squares, full)
    columns = []
    for found in placed_packed(routes[...], regions):
        columns += triple(jnp.sum(jnp.where(found[0] | found[1], inv, 0.0), axis=1, keepdims=True))
    out[:, -128:] = in_lanes(columns, cut)


def early_shape(regions, depth, early):
    return (8 * regions, sum(early) * depth * 5 // 4 + 128)


def pack_early(blocks, routes, regions, depth, full):
    shape = jax.ShapeDtypeStruct(early_shape(regions, depth, EARLY), BF)
    return once(functools.partial(pack_early_kernel, regions, depth, full), shape, routes, *blocks)


def anywhere():
    return pl.BlockSpec(memory_space=pl.ANY)


def expert_kernel(
    regions,
    depth,
    me,
    blocks,
    rows,
    gate_hbm,
    up_hbm,
    down_hbm,
    late_out,
    early_out,
    gate_w,
    up_w,
    down_w,
    acc_g,
    acc_u,
    acc_h,
    hid,
    gate_g,
    up_g,
    scal,
    fold,
    scales,
    sem,
    weight_sems,
):
    width = gate_w.shape[1] // depth
    few = 2 * regions
    cut, lanes = blocks.shape[1:]
    late = late_widths(width, EARLY)
    late_back = late_widths(width, BACK)
    first_block = me[0]
    copy = pltpu.make_async_copy(rows.at[:, rows.shape[1] - 128 :], scales, sem)
    copy.start()

    def lanes_of(step):
        return pl.ds(pl.multiple_of((step + first_block) % depth * width, 128), width)

    def weight_copies(step):
        at = lanes_of(step)
        return [
            pltpu.make_async_copy(gate_hbm.at[:, at, :], gate_w.at[:, at, :], weight_sems.at[0, step]),
            pltpu.make_async_copy(up_hbm.at[:, at, :], up_w.at[:, at, :], weight_sems.at[1, step]),
            pltpu.make_async_copy(down_hbm.at[:, :, at], down_w.at[:, :, at], weight_sems.at[2, step]),
        ]

    for step in range(depth):
        for one in weight_copies(step):
            one.start()
    fold[...] = fold_matrix(regions)
    acc_g[...] = jnp.zeros_like(acc_g)
    acc_u[...] = jnp.zeros_like(acc_u)
    acc_h[...] = jnp.zeros_like(acc_h)

    def body(block, main, rest):
        step = pl.program_id(0)
        at = lanes_of(step)
        for one in weight_copies(step):
            one.wait()
        late_in, late_grad = decode(block[0], late, fold[...])
        pick = fold[pl.ds(pl.multiple_of((step % 4) * few, few), few), :]
        early = jnp.concatenate([main[...], dot(pick, rest[...]).astype(BF)], axis=0)
        rows_in = jnp.concatenate([late_in, early[:, : EARLY[0]]], axis=1)
        rows_grad = jnp.concatenate([late_grad, early[:, EARLY[0] :]], axis=1)
        acc_g[...] += dot(rows_in, gate_w[0, at, :])
        acc_u[...] += dot(rows_in, up_w[0, at, :])
        acc_h[...] += dot(rows_grad, down_w[0, :, at], NT)

    pltpu.emit_pipeline(
        body,
        grid=(depth,),
        in_specs=[
            pl.BlockSpec((1, cut, lanes), lambda z: ((z + first_block) % depth, 0, 0)),
            pl.BlockSpec((cut, sum(EARLY)), lambda z: (0, z)),
            pl.BlockSpec((cut, sum(EARLY)), lambda z: (0, depth + z // 4)),
        ],
    )(blocks, rows, rows)

    copy.wait()
    first = fold[0:few, :]
    inv = jnp.concatenate([from_lanes(scales[...], 0), from_lanes(dot(first, scales[...]), 3)], axis=0)
    gate_raw, up_raw, grad_hidden = acc_g[...], acc_u[...], acc_h[...]
    gate_pre, up_pre = gate_raw * inv, up_raw * inv
    sig = jax.nn.sigmoid(gate_pre)
    act = gate_pre * sig
    hidden = (act * up_pre).astype(BF)
    grad_gate = (grad_hidden * up_pre * sig * (1.0 + gate_pre * (1.0 - sig))).astype(BF)
    grad_up = (grad_hidden * act).astype(BF)
    hid[...] = hidden
    gate_g[...] = grad_gate
    up_g[...] = grad_up
    comb = jnp.sum(hidden.astype(F32) * grad_hidden, axis=1, keepdims=True)
    inner = jnp.sum(grad_gate.astype(F32) * gate_raw + grad_up.astype(F32) * up_raw, axis=1, keepdims=True)
    here = in_lanes(triple(comb[:cut]) + triple(inner[:cut]), cut)
    there = in_lanes([None] * 6 + triple(comb[cut:]) + triple(inner[cut:]), few)
    scal[...] = here + dot(first, there, TN).astype(BF)
    late_lanes = late_out.shape[2]

    def back(late_block, main, rest):
        step = pl.program_id(0)
        at = lanes_of(step)
        moe = dot(hid[...], down_w[0, :, at]).astype(BF)
        grad = (dot(gate_g[...], gate_w[0, at, :], NT) + dot(up_g[...], up_w[0, at, :], NT)).astype(BF)
        both = jnp.concatenate([moe[:, : late_back[0]], grad[:, : late_back[1]]], axis=1)
        late_block[0] = encode(both[:cut], both[cut:], fold[...], late_back)
        both = jnp.concatenate([moe[:, late_back[0] :], grad[:, late_back[1] :]], axis=1)
        main[...] = both[:cut]
        pick = fold[pl.ds(pl.multiple_of((step % 4) * few, few), few), :]
        low = dot(pick, both[cut:], TN).astype(BF)

        @pl.when(step % 4 == 0)
        def _():
            rest[...] = low

        @pl.when(step % 4 > 0)
        def _():
            rest[...] = rest[...] + low

    pltpu.emit_pipeline(
        back,
        grid=(depth,),
        out_specs=[
            pl.BlockSpec((1, cut, late_lanes), lambda z: ((z + first_block) % depth, 0, 0)),
            pl.BlockSpec((cut, sum(BACK)), lambda z: (0, z)),
            pl.BlockSpec((cut, sum(BACK)), lambda z: (0, depth + z // 4)),
        ],
    )(late_out, early_out, early_out)
    pltpu.sync_copy(scal, early_out.at[:, early_out.shape[1] - 128 :])


def expert_part(me, blocks, rows, gate_w, up_w, down_w, regions):
    depth, cut, lanes = blocks.shape
    units = gate_w.shape[2]
    back_lanes = packed_lanes(late_widths(gate_w.shape[1] // depth, BACK))
    total = 10 * regions
    return pl.pallas_call(
        functools.partial(expert_kernel, regions, depth),
        in_specs=[pl.BlockSpec(memory_space=pltpu.SMEM)] + [anywhere()] * 5,
        out_specs=[anywhere()] * 2,
        out_shape=[jax.ShapeDtypeStruct((depth, cut, back_lanes), BF), jax.ShapeDtypeStruct(early_shape(regions, depth, BACK), BF)],
        scratch_shapes=[pltpu.VMEM(w.shape, BF) for w in (gate_w, up_w, down_w)]
        + [pltpu.VMEM((total, units), F32)] * 3
        + [pltpu.VMEM((total, units), BF)] * 3
        + [pltpu.VMEM((cut, 128), BF), pltpu.VMEM((cut, cut), BF), pltpu.VMEM((cut, 128), BF)]
        + [pltpu.SemaphoreType.DMA(()), pltpu.SemaphoreType.DMA((3, depth))],
        compiler_params=params(VMEM_MOST),
    )(me, blocks, rows, gate_w, up_w, down_w)


def scalars(here, routes, weights, regions):
    main, late = placed_packed(routes, regions)
    parts = []
    inner = 0.0
    for k in range(2):
        comb = jnp.where(main[k], from_lanes(here, 0), 0.0) + jnp.where(late[k], from_lanes(here, 6), 0.0)
        part = jnp.where(main[k], from_lanes(here, 3), 0.0) + jnp.where(late[k], from_lanes(here, 9), 0.0)
        parts.append(jnp.sum(comb, axis=0, keepdims=True))
        inner = inner + weights[k : k + 1, :] * jnp.sum(part, axis=0, keepdims=True)
    return parts + [inner]


def combining(routes, weights, regions):
    at = placed(routes, regions)
    weight = jnp.where(at[0], weights[0:1, :], 0.0) + jnp.where(at[1], weights[1:2, :], 0.0)
    high = weight.astype(BF)
    return high, (weight - high.astype(F32)).astype(BF)


def combine_early_kernel(regions, squares, back, routes, weights, out, right, left):
    depth, rows_out, lanes = out.shape
    count = rows_out - EXTRA
    high, low = combining(routes[...], weights[...], regions)
    quarter = depth // 4
    few = 2 * regions
    values = []
    for value in scalars(back[:, -128:], routes[...], weights[...], regions):
        values += triple(value)
    count = routes.shape[1]
    values += [squares[at : at + 1, :count] for at in range(3)]
    extra = in_rows(values, lanes)
    fold = fold_matrix(regions)
    rests = [dot(fold, back[:, (depth + half) * lanes : (depth + half + 1) * lanes]).astype(BF) for half in range(quarter)]
    for z in range(depth):
        part = z % 4
        rest = rests[z // 4][part * few : (part + 1) * few]
        rows = jnp.concatenate([back[:, z * lanes : (z + 1) * lanes], rest], axis=0)
        share = (dot(high, rows, TN) + dot(low, rows, TN)).astype(BF)
        out[z, :count] = share
        out[z, count:] = extra
        if z == depth // 2:
            right[...] = jnp.concatenate([share[: count // 2], extra], axis=0)
            left[...] = jnp.concatenate([share[count // 2 :], extra], axis=0)


def combine_early(early, back, routes, weights, regions, depth):
    count = routes.shape[1]
    squares = early[count:]
    lanes = sum(BACK)
    shapes = [
        jax.ShapeDtypeStruct((depth, count + EXTRA, lanes), BF),
        jax.ShapeDtypeStruct((count // 2 + EXTRA, lanes), BF),
        jax.ShapeDtypeStruct((count // 2 + EXTRA, lanes), BF),
    ]
    return once(functools.partial(combine_early_kernel, regions), shapes, squares, back, routes, weights)


def forward_kernel(for_right, for_left, right, left, right_out, left_out):
    rows = for_right.shape[1]
    count = rows - EXTRA
    arrived = right.shape[0] - EXTRA
    for own, got, out, start in ((for_right, right, right_out, 0), (for_left, left, left_out, count - arrived)):
        if arrived < count:
            out[:count] = own[0, :count]
        spot = slice(start, start + arrived)
        out[spot] = (own[0, spot].astype(F32) + got[:arrived].astype(F32)).astype(BF)
        out[count:] = jnp.concatenate([own[0, count:, :128], got[arrived:, :-128]], axis=1)


def forward(shares, at, right, left):
    depth, rows, lanes = shares.shape
    shape = jax.ShapeDtypeStruct((rows, lanes), BF)
    return pl.pallas_call(
        forward_kernel,
        grid=(1,),
        in_specs=[
            pl.BlockSpec((1, rows, lanes), lambda _: (at, 0, 0)),
            pl.BlockSpec((1, rows, lanes), lambda _: (depth - at, 0, 0)),
            whole(right.shape),
            whole(left.shape),
        ],
        out_specs=[whole((rows, lanes))] * 2,
        out_shape=[shape, shape],
        compiler_params=params(VMEM_SOME),
    )(shares, shares, right, left)


def final_kernel(regions, full, depth, me, back, own, right, left, tok, gain, routes, weights, moe_out, grad_out, comb_out, stack):
    count = tok.shape[0]
    late = late_widths(tok.shape[1], BACK)
    high, low = combining(routes[...], weights[...], regions)
    moe, grad = [dot(high, rows, TN) + dot(low, rows, TN) for rows in decode(back[...], late, fold_matrix(regions))]
    early = own[0, :count].astype(F32) + right[:count].astype(F32) + left[:count].astype(F32)
    moe_out[:, : late[0]] = moe.astype(BF)
    moe_out[:, late[0] :] = early[:, : BACK[0]].astype(BF)
    wide = tok[...].astype(F32)
    stack[0] = own[0, count:, :count].astype(F32)
    for away in range(1, depth):
        source, slot = (left, away - 1) if away <= depth // 2 else (right, depth - away - 1)
        stack[away] = source[count:, slot * 128 : slot * 128 + count].astype(F32)
    total = 0.0
    for z in range(depth):
        total = total + stack[(z - me[0] + depth) % depth]
    comb = [total[3 * k : 3 * k + 1] + total[3 * k + 1 : 3 * k + 2] + total[3 * k + 2 : 3 * k + 3] for k in range(3)]
    comb_out[0:1] = comb[0]
    comb_out[1:2] = comb[1]
    inv = inverse(total[9:10] + total[10:11] + total[11:12], full)
    row = lax.broadcasted_iota(jnp.int32, (8, count), 0)
    columns = jnp.transpose(jnp.where(row == 0, comb[2], jnp.where(row == 1, inv, 0.0)))
    inner, inv = columns[:, 0:1], columns[:, 1:2]
    scaled = gain[...].reshape(1, -1) * jnp.concatenate([grad, early[:, BACK[0] :]], axis=1)
    grad_out[...] = (inv * scaled - wide * (inv * inv * inv * inner / full)).astype(BF)


def final(me, back, shares, right, left, tok, gain, routes, weights, regions, full):
    count, width = tok.shape
    depth, rows, lanes = shares.shape
    shapes = [
        jax.ShapeDtypeStruct((count, width), BF),
        jax.ShapeDtypeStruct((count, width), BF),
        jax.ShapeDtypeStruct((2, count), F32),
    ]
    operands = (back, shares, right, left, tok, gain, routes, weights)
    specs = [whole(operand.shape) for operand in operands]
    specs[1] = pl.BlockSpec((1, rows, lanes), lambda *_: (0, 0, 0))
    return pl.pallas_call(
        functools.partial(final_kernel, regions, full, depth),
        grid_spec=pltpu.PrefetchScalarGridSpec(
            num_scalar_prefetch=1,
            grid=(1,),
            in_specs=specs,
            out_specs=[whole(shape.shape) for shape in shapes],
            scratch_shapes=[pltpu.VMEM((depth, EXTRA, count), F32)],
        ),
        out_shape=shapes,
        compiler_params=params(VMEM_SOME),
    )(me, *operands)


def swap(array, regions):
    split = array.reshape(regions, 8, array.shape[1])
    moved = lax.all_to_all(split, "region", split_axis=0, concat_axis=0, tiled=True)
    return moved.reshape(array.shape)


def hop(array, step):
    depth = lax.axis_size("local")
    return lax.ppermute(array, "local", [(z, (z + step) % depth) for z in range(depth)])


def ring_gather(own):
    half = lax.axis_size("local") // 2
    low, high = own, own
    blocks = [own]
    for _ in range(half - 1):
        low, high = lax.optimization_barrier((hop(low, 1), hop(high, -1)))
        blocks += [low, high]
    cut = (own.shape[0] - EXTRA) // 2
    return blocks + [hop(low[:cut], 1), hop(high[cut:], -1)]


def ring_scatter(shares, right, left, summed):
    for at in range(shares.shape[0] // 2 - 1, -1, -1):
        right, left = hop(right, 1), hop(left, -1)
        if at == shares.shape[0] // 2 - 1:
            summed, _, _ = lax.optimization_barrier((summed, right, left))
        if at:
            right, left = forward(shares, at, right, left)
    return right, left, summed


def on_device(tokens, norm_gain, w_gate, w_up, w_down, routes, combine, grad_out):
    regions = lax.axis_size("region")
    depth = lax.axis_size("local")
    me = lax.axis_index("local").astype(jnp.int32).reshape(1)
    full = depth * tokens.shape[1]
    gain = norm_gain
    routes, weights = routes.T, combine.T
    packed, early = pack(tokens, gain, grad_out, routes, regions)
    around = ring_gather(early)
    arrived, _ = lax.optimization_barrier((swap(packed, regions), around[4]))
    blocks = lax.all_gather(arrived, "local")
    early_rows = pack_early(around, routes, regions, depth, full)
    rows = swap(early_rows, regions)
    partial, back_rows = expert_part(me, blocks, rows, w_gate, w_up, w_down, regions)
    summed = lax.psum_scatter(partial, "local", scatter_dimension=0)
    shares, right, left = combine_early(early, swap(back_rows, regions), routes, weights, regions, depth)
    right, left, summed = ring_scatter(shares, right, left, summed)
    moe, grad, comb = final(me, swap(summed, regions), shares, right, left, tokens, gain, routes, weights, regions, full)
    return moe, grad, comb.T


def solution(mesh):
    specs = (
        P("region", "local"),
        P("local"),
        P("region", None, "local"),
        P("region", None, "local"),
        P("region", "local", None),
        P("region", None),
        P("region", None),
        P("region", "local"),
    )
    return jax.shard_map(
        on_device,
        mesh=mesh,
        in_specs=specs,
        out_specs=(P("region", "local"), P("region", "local"), P("region", None)),
        check_vma=False,
    )
```
